512 devices in a mesh: enc: 16 (over x, z_hi), seq: 8 (over y, core), tp: 4 (over z_lo).
Axes of the slice: x: 4, y: 4, z: 16 (z_hi: 4, z_lo: 4; z = z_hi * 4 + z_lo), core: 2. Of those that a mesh axis runs over, the one named last changes fastest.
Arguments:
- visual_key_value: bfloat16 [16, 16, 256, 2048], P(None, 'seq', 'enc', 'tp'), may hold values from -4.5 to 4.5
- patch_blocks: int32 [16, 16], P('enc'), may hold values from 1 to 8
- queries: bfloat16 [16, 16, 32, 8192], P('enc', 'seq', None, 'tp'), may hold values from -113 to 113
- suffix_key_value: bfloat16 [16, 16, 32, 2048], P('enc', 'seq', None, 'tp'), may hold values from -6 to 6
- suffix_hidden_state: bfloat16 [16, 16, 32, 8192], P('enc', 'seq', None, 'tp'), may hold values from -6 to 6
- down_weight: bfloat16 [8192, 128], P('tp'), may hold values from -0.0625 to 0.0625
- up_weight: bfloat16 [128, 8192], P(None, 'tp'), may hold values from -1.5 to 1.5
- question_adapter: int32 [16, 16], P('enc', 'seq'), may hold values from 0 to 7
- suffix_token_length: int32 [16, 16], P('enc', 'seq'), may hold values from 1 to 32
Outputs:
- context: bfloat16 [16, 16, 32, 8192], P('enc', 'seq', None, 'tp')
The draws below stay inside these ranges and needn't reach their ends.
All inputs are finite; a program needn't handle non-finite values.
Results may differ from the reference program's by a relative error of at most 0.0087.
Values may be sent and summed in bfloat16 or wider, within the bound.
A program may use at most 64 MiB of HBM per device.

```python
import math
import jax
import jax.numpy as jnp
from jax import lax

MODEL_WIDTH = 8192
QUERY_HEADS = 64
KV_HEADS = 8
HEAD_SIZE = 128
ADAPTER_RANK = 16
ADAPTER_COUNT = 8
PAGES = 16
PAGE_TOK = 256
QTOK = 32
DOCS = 16
QUESTIONS = 16
KVW = 2048


def base_keys(key):
    values = jax.random.normal(jax.random.fold_in(key, 11), (DOCS, PAGES, PAGE_TOK, KVW), jnp.float32)
    return jnp.clip(values, -4.5, 4.5)


def draw_visual_key_value(key, part):
    values = base_keys(key)
    return values.astype(jnp.bfloat16)


def draw_queries(key, part):
    values = jax.random.normal(jax.random.fold_in(key, 23), (DOCS, QUESTIONS, QTOK, QUERY_HEADS * HEAD_SIZE), jnp.float32)
    values = jnp.clip(values, -4.5, 4.5)
    return values.astype(jnp.bfloat16)


def place_ends(values, own_key, least, largest):
    longest = values.shape.index(max(values.shape))
    spots = []
    for shift in (0, 1):
        where = [jax.random.randint(jax.random.fold_in(own_key, axis), (), 0, length) for axis, length in enumerate(values.shape)]
        where[longest] = (where[longest] + shift) % values.shape[longest]
        spots.append(tuple(where))
    return values.at[spots[0]].set(least).at[spots[1]].set(largest)


def block_scale(own_key, extent, cuts, smallest, high):
    factor_of = 1.0
    for axis_at, parts in cuts:
        draws = jax.random.uniform(jax.random.fold_in(jax.random.fold_in(own_key, 6), axis_at), (parts,), jnp.float32, smallest / len(cuts), high / len(cuts))
        factor_of = factor_of * jnp.repeat(jnp.exp(draws), extent[axis_at] // parts).reshape((-1,) + (1,) * (len(extent) - 1 - axis_at))
    return factor_of


def noise(stream_key, extent, scale, limit, pieces=(), kind=jnp.bfloat16):
    drawn = jax.random.normal(stream_key, extent, jnp.float32) * scale
    if len(pieces) > 0:
        drawn = block_scale(stream_key, extent, pieces, -0.22, 0.18) * drawn
    return jnp.clip(drawn, min=-limit, max=limit).astype(kind)


def setup_inputs(seed: int = 0) -> dict:
    keys = jax.random.split(jax.random.key(seed), 10)
    visual_key_value = draw_visual_key_value(jax.random.fold_in(keys[9], 71), 0)
    patch_blocks = place_ends(jax.random.randint(keys[1], (DOCS, PAGES), 1, 9), jax.random.fold_in(keys[1], 1), 1, 8).astype(jnp.int32)
    queries = draw_queries(jax.random.fold_in(keys[9], 71), 0)
    suffix_key_value = noise(keys[3], (DOCS, QUESTIONS, QTOK, KVW), 1.4, 6.0, ((0, 16), (1, 8), (3, 4)))
    suffix_hidden_state = noise(keys[4], (DOCS, QUESTIONS, QTOK, MODEL_WIDTH), 1.0, 6.0, ((0, 16), (1, 8), (3, 4)))
    down_weight = noise(keys[5], (MODEL_WIDTH, ADAPTER_COUNT * ADAPTER_RANK), MODEL_WIDTH ** -0.5, 0.0625, ((0, 4),))
    up_weight = noise(keys[6], (ADAPTER_COUNT * ADAPTER_RANK, QUERY_HEADS * HEAD_SIZE), ADAPTER_RANK ** -0.5, 1.5, ((1, 4),))
    question_adapter = place_ends(jax.random.randint(keys[7], (DOCS, QUESTIONS), 0, ADAPTER_COUNT), jax.random.fold_in(keys[7], 1), 0, ADAPTER_COUNT - 1).astype(jnp.int32)
    suffix_token_length = place_ends(jax.random.randint(keys[8], (DOCS, QUESTIONS), 1, QTOK + 1), jax.random.fold_in(keys[8], 1), 1, QTOK).astype(jnp.int32)
    return dict(visual_key_value=visual_key_value, patch_blocks=patch_blocks, queries=queries, suffix_key_value=suffix_key_value, suffix_hidden_state=suffix_hidden_state, down_weight=down_weight, up_weight=up_weight, question_adapter=question_adapter, suffix_token_length=suffix_token_length)


NEG_BIG = -1e+30
ADAPTER_SCALE = 2.0

def reference(visual_key_value, patch_blocks, queries, suffix_key_value, suffix_hidden_state, down_weight, up_weight, question_adapter, suffix_token_length):
    head_group = QUERY_HEADS // KV_HEADS
    inverse = 1.0 / math.sqrt(HEAD_SIZE)
    row_totals = DOCS * QUESTIONS * QTOK
    asked_rows = QUESTIONS * QTOK
    key_count = PAGES * PAGE_TOK
    hidden_state_rows = suffix_hidden_state.reshape(row_totals, MODEL_WIDTH)
    reduced_features = jnp.dot(hidden_state_rows, down_weight, preferred_element_type=jnp.float32)
    owning_question = jnp.arange(ADAPTER_COUNT * ADAPTER_RANK, dtype=jnp.int32) // ADAPTER_RANK
    row_ids = jnp.broadcast_to(question_adapter[:, :, None], (DOCS, QUESTIONS, QTOK)).reshape(row_totals, 1)
    selected_adapter = jnp.where(owning_question[None, :] == row_ids, reduced_features, 0.0).astype(jnp.bfloat16)
    raised_features = jnp.dot(selected_adapter, up_weight, preferred_element_type=jnp.float32)
    query_matrix = (queries.reshape(row_totals, QUERY_HEADS * HEAD_SIZE).astype(jnp.float32) + ADAPTER_SCALE * raised_features).astype(jnp.bfloat16)
    query_matrix = query_matrix.reshape(DOCS, asked_rows, KV_HEADS, head_group, HEAD_SIZE)
    visual = visual_key_value.reshape(DOCS, key_count, KV_HEADS, 2, HEAD_SIZE)
    token_pos = jnp.arange(PAGE_TOK, dtype=jnp.int32)
    live_keys = (8 * token_pos[None, None, :] < patch_blocks[:, :, None] * PAGE_TOK).reshape(DOCS, key_count)
    suffix_pairs = suffix_key_value.reshape(DOCS, QUESTIONS, QTOK, KV_HEADS, 2, HEAD_SIZE)
    positions = jnp.arange(QTOK, dtype=jnp.int32)
    causal = positions[None, :] <= positions[:, None]
    within = positions[None, None, :] < suffix_token_length[:, :, None]
    own_valid = causal[None, None, :, :] & within[:, :, None, :]

    def per_doc(doc_inputs):
        query_doc, visual_doc, live_doc, pairs_doc, valid_doc = doc_inputs

        def per_head(head_inputs):
            query_head, visual_head, pairs_head = head_inputs
            query_float = query_head.astype(jnp.float32)
            visual_scores = jnp.einsum('ngd,ld->ngl', query_float, visual_head[:, 0, :].astype(jnp.float32)) * inverse
            visual_scores = jnp.where(live_doc[None, None, :], visual_scores, NEG_BIG)
            query_split = query_float.reshape(QUESTIONS, QTOK, head_group, HEAD_SIZE)
            suffix_scores = jnp.einsum('qigd,qjd->qigj', query_split, pairs_head[:, :, 0, :].astype(jnp.float32)) * inverse
            suffix_mask = valid_doc[:, :, None, :]
            suffix_scores = jnp.where(suffix_mask, suffix_scores, NEG_BIG)
            row_peak = jnp.maximum(visual_scores.max(axis=-1), suffix_scores.max(axis=-1).reshape(asked_rows, head_group))
            visual_weights = jnp.where(live_doc[None, None, :], jnp.exp(visual_scores - row_peak[:, :, None]), 0.0)
            peak_split = row_peak.reshape(QUESTIONS, QTOK, head_group)
            suffix_weights = jnp.where(suffix_mask, jnp.exp(suffix_scores - peak_split[:, :, :, None]), 0.0)
            denominator = visual_weights.sum(axis=-1) + suffix_weights.sum(axis=-1).reshape(asked_rows, head_group)
            visual_rounded = lax.optimization_barrier(visual_weights.astype(jnp.bfloat16)).astype(jnp.float32)
            suffix_rounded = lax.optimization_barrier(suffix_weights.astype(jnp.bfloat16)).astype(jnp.float32)
            numerators = jnp.einsum('ngl,ld->ngd', visual_rounded, visual_head[:, 1, :].astype(jnp.float32))
            numerators = numerators + jnp.einsum('qigj,qjd->qigd', suffix_rounded, pairs_head[:, :, 1, :].astype(jnp.float32)).reshape(asked_rows, head_group, HEAD_SIZE)
            return numerators / denominator[:, :, None]
        heads_out = lax.map(per_head, (jnp.moveaxis(query_doc, 1, 0), jnp.moveaxis(visual_doc, 1, 0), jnp.moveaxis(pairs_doc, 2, 0)))
        return jnp.moveaxis(heads_out, 0, 1)
    outputs = lax.map(per_doc, (query_matrix, visual, live_keys, suffix_pairs, own_valid))
    outputs = outputs.reshape(DOCS, QUESTIONS, QTOK, QUERY_HEADS * HEAD_SIZE)
    kept_rows = positions[None, None, :] < suffix_token_length[:, :, None]
    return jnp.where(kept_rows[:, :, :, None], outputs, 0.0).astype(jnp.bfloat16)
```

```python
import math

import jax
import jax.numpy as jnp
from jax import lax
from jax.experimental import pallas as pl
from jax.experimental.pallas import tpu as pltpu
from jax.sharding import PartitionSpec as P

MESH = pl.DeviceIdType.MESH
HEAD_SIZE = 128
ADAPTER_RANK = 16
ADAPTER_SCALE = 2.0
NEG_BIG = -1e30
NX, NZ, NY = 4, 4, 4
SLOTS = NX * NZ
GROUP = 4
KEYS = GROUP * 64
COLS = 1024
BLOCK = 256
EXP2_SCALE = math.log2(math.e) / math.sqrt(HEAD_SIZE)
OFFSETS = (
    [(0, 0), (1, 0), (3, 0), (2, 0)]
    + [(dx, dz) for dx in (2, 3, 1, 0) for dz in (1, 3)]
    + [(dx, 2) for dx in (2, 3, 1, 0)]
)


def spread(rows):
    for shift in (64, 32, 16):
        rows = rows + pltpu.roll(rows, shift, 1)
    return rows


def kernel(
    blocks_ref,
    adapter_ref,
    length_ref,
    visual,
    queries,
    suffix,
    hidden,
    down,
    up,
    out,
    kv,
    sx,
    qx,
    qfull,
    qt,
    acc,
    peak,
    total,
    res,
    hidden_v,
    down_v,
    up_v,
    queries_v,
    tp_send,
    tp_recv,
    len_tile,
    source_of,
    load_sem,
    a2a_send,
    a2a_recv,
    y_send,
    y_recv,
    tp_ssem,
    tp_rsem,
    sib_ssem,
    sib_rsem,
    out_sem,
):
    e, s, t = lax.axis_index("enc"), lax.axis_index("seq"), lax.axis_index("tp")
    x, z = e // NZ, e % NZ
    y, c = s // 2, s % 2
    oc = 1 - c

    def enc_at(dx, dz):
        return ((x + dx) % NX) * NZ + (z + dz) % NZ

    def y_at(dy):
        return (e, ((y + dy) % NY) * 2 + c, t)

    sibling = (e, y * 2 + oc, t)

    loads = [
        pltpu.make_async_copy(src, dst, load_sem.at[i])
        for i, (src, dst) in enumerate(
            ((hidden, hidden_v), (down, down_v), (up, up_v), (queries, queries_v))
        )
    ]
    for load in loads:
        load.start()
    own_cols = pl.ds(pl.multiple_of(c * 256, 256), 256)
    sib_cols = pl.ds(pl.multiple_of(oc * 256, 256), 256)
    own_tile = pltpu.make_async_copy(
        visual.at[e, :, :, own_cols], kv.at[0, 0, pl.ds(2 * c, 2)], load_sem.at[4]
    )
    own_tile.start()
    own_suffix = pltpu.make_async_copy(
        suffix.at[:, :, own_cols], sx.at[c], load_sem.at[5]
    )
    own_suffix.start()

    barrier = pltpu.get_barrier_semaphore()
    peers = [sibling, y_at(1), y_at(3)]
    peers += [(e, s, (t + k) % 4) for k in (1, 2, 3)]
    for dx, dz in OFFSETS[1:]:
        for core in (c, oc):
            peers.append((enc_at(dx, dz), y * 2 + core, t))
    for peer in peers:
        pl.semaphore_signal(barrier, inc=1, device_id=peer, device_id_type=MESH)

    for j, (dx, dz) in enumerate(OFFSETS):
        source_of[j] = enc_at(NX - dx, NZ - dz)

    lane = lax.broadcasted_iota(jnp.int32, (8, 128), 1)
    loads[0].wait()
    loads[1].wait()
    lowered = jnp.dot(hidden_v[...], down_v[...], preferred_element_type=jnp.float32)
    packed = jnp.zeros((8, 128), jnp.float32)
    for g in range(8):
        own_adapter = adapter_ref[0, g // 4]
        rows = jnp.where(lane // ADAPTER_RANK == own_adapter, lowered[8 * g : 8 * g + 8], 0.0)
        packed = jnp.where(lane // ADAPTER_RANK == g, spread(rows), packed)
    tp_send[...] = packed
    len_tile[c] = jnp.where((lane // 32) % 2 == 0, length_ref[0, 0], length_ref[0, 1]).astype(
        jnp.float32
    )

    pl.semaphore_wait(barrier, len(peers))

    def remote(src, dst, ssem, rsem, device):
        return pltpu.make_async_remote_copy(
            src_ref=src,
            dst_ref=dst,
            send_sem=ssem,
            recv_sem=rsem,
            device_id=device,
            device_id_type=MESH,
        )

    tp_copies = [
        remote(
            tp_send, tp_recv.at[k - 1], tp_ssem.at[k - 1], tp_rsem.at[k - 1], (e, s, (t + k) % 4)
        )
        for k in (1, 2, 3)
    ]
    for copy in tp_copies:
        copy.start()

    def tile_send(j, core, cols):
        target = enc_at(*OFFSETS[j])
        return remote(
            visual.at[target, :, :, cols],
            kv.at[0, j, pl.ds(2 * c, 2)],
            a2a_send.at[j, core],
            a2a_recv.at[j, c],
            (target, y * 2 + core, t),
        )

    tile_send(0, oc, sib_cols).start()
    suffix_copy = remote(
        suffix.at[:, :, sib_cols], sx.at[c], sib_ssem.at[0], sib_rsem.at[0], sibling
    )
    suffix_copy.start()
    len_copy = remote(len_tile.at[c], len_tile.at[c], sib_ssem.at[1], sib_rsem.at[1], sibling)
    len_copy.start()
    for j in range(1, SLOTS):
        tile_send(j, c, own_cols).start()
        tile_send(j, oc, sib_cols).start()

    def tile_wait(j, core):
        dst = kv.at[0, j, pl.ds(2 * core, 2)]
        remote(dst, dst, a2a_send.at[j, core], a2a_recv.at[j, core], sibling).wait_recv()

    def y_copy(way, j):
        return remote(
            kv.at[0, j],
            kv.at[1 + way, j],
            y_send.at[way, j],
            y_recv.at[way, j],
            y_at(1 if way == 0 else 3),
        )

    def y_relay(j):
        way = j % 2
        return remote(
            kv.at[1 + way, j],
            kv.at[3, j],
            y_send.at[2, j],
            y_recv.at[2, j],
            (e, ((y + 1 + 2 * way) % NY) * 2 + c, t),
        )

    def y_wait(way, j):
        dst = kv.at[1 + way, j]
        remote(dst, dst, y_send.at[way, j], y_recv.at[way, j], sibling).wait_recv()

    def forward(j):
        y_copy(0, j).start()
        y_copy(1, j).start()

    def relay(j):
        y_wait(j % 2, j)
        y_relay(j).start()

    own_tile.wait()
    tile_wait(0, oc)
    forward(0)

    for copy in tp_copies:
        copy.wait_recv()
    packed = tp_send[...] + tp_recv[0] + tp_recv[1] + tp_recv[2]
    picked = []
    for g in range(8):
        own_adapter = adapter_ref[0, g // 4]
        rows = spread(jnp.where(lane // ADAPTER_RANK == g, packed, 0.0))
        picked.append(jnp.where(lane // ADAPTER_RANK == own_adapter, rows, 0.0))
    picked = jnp.concatenate(picked, axis=0).astype(jnp.bfloat16)
    loads[2].wait()
    loads[3].wait()
    for n in range(8):
        at = slice(n * 256, (n + 1) * 256)
        raised = jnp.dot(picked, up_v[:, at], preferred_element_type=jnp.float32)
        qfull[:, at] = (
            queries_v[:, at].astype(jnp.float32) + ADAPTER_SCALE * raised
        ).astype(jnp.bfloat16)
    own_half = pl.ds(pl.multiple_of(c * COLS, COLS), COLS)
    sib_half = pl.ds(pl.multiple_of(oc * COLS, COLS), COLS)
    query_copy = remote(
        qfull.at[:, sib_half], qx.at[c], sib_ssem.at[2], sib_rsem.at[2], sibling
    )
    query_copy.start()
    qx[c] = qfull[:, own_half]

    for j in range(1, GROUP):
        tile_wait(j, 0)
        tile_wait(j, 1)
        forward(j)
    for j in range(2):
        relay(j)

    for index, dst in ((0, sx.at[oc]), (1, len_tile.at[oc]), (2, qx.at[oc])):
        remote(dst, dst, sib_ssem.at[index], sib_rsem.at[index], sibling).wait_recv()
    own_suffix.wait()

    for g in range(8):
        rows = qx[:, :, g * 128 : (g + 1) * 128].reshape(128, 128)
        qt[:, g * 128 : (g + 1) * 128] = rows.T

    lengths = jnp.where(lane // 64 == 0, len_tile[0], len_tile[1])[0:1].astype(jnp.int32)
    key_at = lax.broadcasted_iota(jnp.int32, (128, 128), 0)
    col_at = lax.broadcasted_iota(jnp.int32, (128, 128), 1)
    limit = jnp.minimum(col_at % 32, lengths - 1)
    seen = (key_at // 32 == col_at // 32) & (key_at % 32 <= limit)
    keys = sx[:, :, :, 0:128].reshape(128, 128)
    values_t = sx[:, :, :, 128:256].reshape(128, 128).T
    for g in range(8):
        at = slice(g * 128, (g + 1) * 128)
        scores = jnp.dot(keys, qt[:, at], preferred_element_type=jnp.float32)
        scores = jnp.where(seen, scores, NEG_BIG)
        top = scores.max(axis=0, keepdims=True)
        weights = jnp.where(seen, jnp.exp2((scores - top) * EXP2_SCALE), 0.0)
        peak[:, at] = top
        total[:, at] = weights.sum(axis=0, keepdims=True)
        acc[:, at] = jnp.dot(
            values_t, weights.astype(jnp.bfloat16), preferred_element_type=jnp.float32
        )

    def attend(r, g):
        tile = kv.at[r, pl.ds(g * GROUP, GROUP)]
        keys = tile[:, :, :, 0:128].reshape(KEYS, 128)
        values_t = tile[:, :, :, 128:256].reshape(KEYS, 128).T
        from_y = (y + jnp.where(r == 0, 0, jnp.where(r == 1, 3, jnp.where(r == 2, 1, 2)))) % NY
        bias = []
        for i in range(GROUP * 4):
            held = blocks_ref[0, from_y * 4 + i % 4]
            live = source_of[g * GROUP + i // 4] < 2 * held
            bias.append(jnp.where(live, 0.0, NEG_BIG))
        for b in range(COLS // BLOCK):
            at = slice(b * BLOCK, (b + 1) * BLOCK)
            scores = jnp.dot(keys, qt[:, at], preferred_element_type=jnp.float32)
            before = peak[:, at]
            top = before
            for i in range(GROUP * 4):
                part = scores[16 * i : 16 * i + 16].max(axis=0, keepdims=True)
                top = jnp.maximum(top, part + bias[i])
            shrink = jnp.exp2((before - top) * EXP2_SCALE)
            parts = []
            added = jnp.zeros((16, BLOCK), jnp.float32)
            for i in range(GROUP * 4):
                part = jnp.exp2((scores[16 * i : 16 * i + 16] - (top - bias[i])) * EXP2_SCALE)
                added = added + part
                parts.append(part.astype(jnp.bfloat16))
            peak[:, at] = top
            total[:, at] = total[:, at] * shrink + added.sum(axis=0, keepdims=True)
            acc[:, at] = acc[:, at] * shrink + jnp.dot(
                values_t, jnp.concatenate(parts, axis=0), preferred_element_type=jnp.float32
            )

    def step(k, _):
        @pl.when(k < SLOTS)
        def _():
            tile_wait(k, 0)
            tile_wait(k, 1)
            forward(k)

        @pl.when(k < SLOTS + 2)
        def _():
            relay(k - 2)

        unit = k - GROUP
        g, r = unit // 4, unit % 4
        for i in range(GROUP):
            j = g * GROUP + i

            @pl.when((r == 1 + (1 - i % 2)) | (r == 3))
            def _():
                way = jnp.where(r == 3, 2, 1 - i % 2)
                y_wait(way, j)

        attend(r, g)
        return 0

    lax.fori_loop(GROUP, SLOTS + GROUP, step, 0)

    keep = lax.broadcasted_iota(jnp.int32, (1, 128), 1) % 32 < lengths
    for g in range(8):
        at = slice(g * 128, (g + 1) * 128)
        rows = jnp.where(keep, acc[:, at] / total[:, at], 0.0).T
        res[:, :, at] = rows.reshape(2, 64, 128).astype(jnp.bfloat16)
    out_copy = remote(
        res.at[oc], out.at[:, own_half], sib_ssem.at[3], sib_rsem.at[3], sibling
    )
    out_copy.start()
    local_out = pltpu.make_async_copy(res.at[c], out.at[:, own_half], out_sem)
    local_out.start()

    def drain(j, _):
        for core in (0, 1):

            @pl.when((j > 0) | (core == oc))
            def _():
                src = kv.at[0, j, pl.ds(2 * core, 2)]
                remote(src, src, a2a_send.at[j, core], a2a_recv.at[j, core], sibling).wait_send()

        for way in (0, 1, 2):
            src = kv.at[1 + way, j]
            remote(src, src, y_send.at[way, j], y_recv.at[way, j], sibling).wait_send()
        return 0

    lax.fori_loop(0, SLOTS, drain, 0)
    for copy in tp_copies + [suffix_copy, len_copy, query_copy]:
        copy.wait_send()
    local_out.wait()
    out_copy.wait_send()
    arrived = out.at[:, sib_half]
    remote(arrived, arrived, sib_ssem.at[3], sib_rsem.at[3], sibling).wait_recv()


def per_device(
    visual_key_value,
    patch_blocks,
    queries,
    suffix_key_value,
    suffix_hidden_state,
    down_weight,
    up_weight,
    question_adapter,
    suffix_token_length,
):
    bf16, f32 = jnp.bfloat16, jnp.float32
    asked, positions, width = queries.shape[1:]
    rows = asked * positions
    dma = pltpu.SemaphoreType.DMA
    smem = pl.BlockSpec(memory_space=pltpu.SMEM)
    hbm = pl.BlockSpec(memory_space=pl.ANY)
    result = pl.pallas_call(
        kernel,
        name="attention",
        out_shape=jax.ShapeDtypeStruct((rows, width), bf16),
        in_specs=[smem] * 3 + [hbm] * 6,
        out_specs=hbm,
        scratch_shapes=[
            pltpu.VMEM((4, SLOTS, 4, 16, 256), bf16),
            pltpu.VMEM((2, 2, 32, 256), bf16),
            pltpu.VMEM((2, rows, COLS), bf16),
            pltpu.VMEM((rows, width), bf16),
            pltpu.VMEM((HEAD_SIZE, COLS), bf16),
            pltpu.VMEM((HEAD_SIZE, COLS), f32),
            pltpu.VMEM((1, COLS), f32),
            pltpu.VMEM((1, COLS), f32),
            pltpu.VMEM((2, rows, COLS), bf16),
            pltpu.VMEM((rows, width), bf16),
            pltpu.VMEM(down_weight.shape, bf16),
            pltpu.VMEM(up_weight.shape, bf16),
            pltpu.VMEM((rows, width), bf16),
            pltpu.VMEM((8, 128), f32),
            pltpu.VMEM((3, 8, 128), f32),
            pltpu.VMEM((2, 8, 128), f32),
            pltpu.SMEM((SLOTS,), jnp.int32),
            dma((6,)),
            dma((SLOTS, 2)),
            dma((SLOTS, 2)),
            dma((3, SLOTS)),
            dma((3, SLOTS)),
            dma((3,)),
            dma((3,)),
            dma((4,)),
            dma((4,)),
            dma,
        ],
        compiler_params=pltpu.CompilerParams(
            collective_id=0, has_side_effects=True, vmem_limit_bytes=56 << 20
        ),
    )(
        patch_blocks,
        question_adapter,
        suffix_token_length,
        visual_key_value,
        queries.reshape(rows, width),
        suffix_key_value.reshape(asked, positions, -1),
        suffix_hidden_state.reshape(rows, width),
        down_weight,
        up_weight,
    )
    return result.reshape(queries.shape)


def solution(mesh):
    placed = (
        P(None, "seq", "enc", "tp"),
        P("enc", None),
        P("enc", "seq", None, "tp"),
        P("enc", "seq", None, "tp"),
        P("enc", "seq", None, "tp"),
        P("tp", None),
        P(None, "tp"),
        P("enc", "seq"),
        P("enc", "seq"),
    )
    return jax.shard_map(
        per_device,
        mesh=mesh,
        in_specs=placed,
        out_specs=P("enc", "seq", None, "tp"),
        check_vma=False,
    )
```

```python
import math

import jax
import jax.numpy as jnp
from jax import lax
from jax.experimental import pallas as pl
from jax.experimental.pallas import tpu as pltpu
from jax.sharding import PartitionSpec as P

MESH = pl.DeviceIdType.MESH
HEAD_SIZE = 128
ADAPTER_RANK = 16
ADAPTER_SCALE = 2.0
NEG_BIG = -1e30
NX, NZ, NY = 4, 4, 4
SLOTS = NX * NZ
GROUP = 4
KEYS = GROUP * 64
COLS = 1024
BLOCK = 128
EXP2_SCALE = math.log2(math.e) / math.sqrt(HEAD_SIZE)
HERE = [(0, 0), (1, 0), (3, 0), (2, 0)]
NEAR = [(dx, dz) for dx in (2, 3, 1, 0) for dz in (1, 3)]
FAR = [(dx, 2) for dx in (2, 3, 1, 0)]
OFFSETS = HERE + NEAR + FAR
FIRST_FAR = len(HERE + NEAR)
LATE = GROUP + 1


def spread(rows):
    for shift in (64, 32, 16):
        rows = rows + pltpu.roll(rows, shift, 1)
    return rows


def kernel(
    blocks,
    adapter,
    length,
    visual,
    queries,
    suffix,
    hidden,
    down,
    up,
    out,
    kv,
    sx,
    qx,
    qfull,
    qt,
    acc,
    peak,
    total,
    res,
    hidden_v,
    down_v,
    up_v,
    queries_v,
    tp_send,
    tp_recv,
    len_tile,
    source_of,
    blocks_ref,
    adapter_ref,
    length_ref,
    load_sem,
    a2a_send,
    a2a_recv,
    y_send,
    y_recv,
    tp_ssem,
    tp_rsem,
    sib_ssem,
    sib_rsem,
    out_ssem,
    out_rsem,
    far_ready,
):
    e, s, t = lax.axis_index("enc"), lax.axis_index("seq"), lax.axis_index("tp")
    x, z = e // NZ, e % NZ
    y, c = s // 2, s % 2
    oc = 1 - c

    def enc_at(dx, dz):
        return ((x + dx) % NX) * NZ + (z + dz) % NZ

    def y_at(dy):
        return (e, ((y + dy) % NY) * 2 + c, t)

    sibling = (e, y * 2 + oc, t)

    barrier = pltpu.get_barrier_semaphore()
    peers = [sibling, y_at(1), y_at(2), y_at(3)]
    peers += [(e, s, (t + k) % 4) for k in (1, 2, 3)]
    for dx, dz in (HERE + NEAR)[1:]:
        for core in (c, oc):
            peers.append((enc_at(dx, dz), y * 2 + core, t))
    for peer in peers:
        pl.semaphore_signal(barrier, inc=1, device_id=peer, device_id_type=MESH)

    loads = [
        pltpu.make_async_copy(src, dst, load_sem.at[i])
        for i, (src, dst) in enumerate(
            ((hidden, hidden_v), (down, down_v), (up, up_v), (queries, queries_v))
        )
    ]
    for load in loads:
        load.start()
    scalars = [
        pltpu.make_async_copy(src, dst, load_sem.at[6 + i])
        for i, (src, dst) in enumerate(
            ((blocks, blocks_ref), (adapter, adapter_ref), (length, length_ref))
        )
    ]
    for load in scalars:
        load.start()
    own_cols = pl.ds(pl.multiple_of(c * 256, 256), 256)
    sib_cols = pl.ds(pl.multiple_of(oc * 256, 256), 256)
    own_tile = pltpu.make_async_copy(
        visual.at[e, :, :, own_cols], kv.at[0, 0, pl.ds(2 * c, 2)], load_sem.at[4]
    )
    own_tile.start()
    own_suffix = pltpu.make_async_copy(
        suffix.at[:, :, own_cols], sx.at[c], load_sem.at[5]
    )
    own_suffix.start()

    for j, (dx, dz) in enumerate(OFFSETS):
        source_of[j] = enc_at(NX - dx, NZ - dz)

    lane = lax.broadcasted_iota(jnp.int32, (8, 128), 1)
    for load in [loads[0], loads[1], *scalars]:
        load.wait()
    lowered = jnp.dot(hidden_v[...], down_v[...], preferred_element_type=jnp.float32)
    packed = jnp.zeros((8, 128), jnp.float32)
    for g in range(8):
        own_adapter = adapter_ref[0, g // 4]
        rows = jnp.where(lane // ADAPTER_RANK == own_adapter, lowered[8 * g : 8 * g + 8], 0.0)
        packed = jnp.where(lane // ADAPTER_RANK == g, spread(rows), packed)
    tp_send[...] = packed
    len_tile[c] = jnp.where((lane // 32) % 2 == 0, length_ref[0, 0], length_ref[0, 1]).astype(
        jnp.float32
    )

    pl.semaphore_wait(barrier, len(peers))

    def remote(src, dst, ssem, rsem, device):
        return pltpu.make_async_remote_copy(
            src_ref=src,
            dst_ref=dst,
            send_sem=ssem,
            recv_sem=rsem,
            device_id=device,
            device_id_type=MESH,
        )

    tp_copies = [
        remote(
            tp_send, tp_recv.at[k - 1], tp_ssem.at[k - 1], tp_rsem.at[k - 1], (e, s, (t + k) % 4)
        )
        for k in (1, 2, 3)
    ]
    for copy in tp_copies:
        copy.start()

    def tile_send(dx, dz, j, core, cols):
        target = enc_at(dx, dz)
        return remote(
            visual.at[target, :, :, cols],
            kv.at[0, j, pl.ds(2 * c, 2)],
            a2a_send.at[j, core],
            a2a_recv.at[j, c],
            (target, y * 2 + core, t),
        )

    tile_send(0, 0, 0, oc, sib_cols).start()
    suffix_copy = remote(
        suffix.at[:, :, sib_cols], sx.at[c], sib_ssem.at[0], sib_rsem.at[0], sibling
    )
    suffix_copy.start()
    len_copy = remote(len_tile.at[c], len_tile.at[c], sib_ssem.at[1], sib_rsem.at[1], sibling)
    len_copy.start()
    for j in range(1, GROUP):
        tile_send(*OFFSETS[j], j, c, own_cols).start()
        tile_send(*OFFSETS[j], j, oc, sib_cols).start()
    for j in range(GROUP, FIRST_FAR):
        tile_send(*OFFSETS[j], j, c, own_cols).start()
        tile_send(*OFFSETS[j], j, oc, sib_cols).start()
    pl.semaphore_signal(
        far_ready, inc=1, device_id=(enc_at(0, NZ - 1), s, t), device_id_type=MESH
    )

    def far_sends():
        for j in range(FIRST_FAR, SLOTS):
            tile_send(*OFFSETS[j], j, c, own_cols).start()
            tile_send(*OFFSETS[j], j, oc, sib_cols).start()

    inner = (t == 1) | (t == 2)

    def tile_wait(j, core):
        dst = kv.at[0, j, pl.ds(2 * core, 2)]
        remote(dst, dst, a2a_send.at[j, core], a2a_recv.at[j, core], sibling).wait_recv()

    def y_copy(way, j):
        return remote(
            kv.at[0, j],
            kv.at[1 + way, j],
            y_send.at[way, j],
            y_recv.at[way, j],
            y_at(1 if way == 0 else 3),
        )

    def y_relay(j):
        way = j % 2
        return remote(
            kv.at[1 + way, j],
            kv.at[3, j],
            y_send.at[2, j],
            y_recv.at[2, j],
            (e, ((y + 1 + 2 * way) % NY) * 2 + c, t),
        )

    def y_across(j):
        return remote(
            kv.at[0, j], kv.at[3, j], y_send.at[2, j], y_recv.at[2, j], y_at(2)
        )

    def y_wait(way, j):
        dst = kv.at[1 + way, j]
        remote(dst, dst, y_send.at[way, j], y_recv.at[way, j], sibling).wait_recv()

    def forward(j):
        y_copy(0, j).start()
        y_copy(1, j).start()

    def relay(j):
        y_wait(j % 2, j)
        y_relay(j).start()

    own_tile.wait()
    tile_wait(0, oc)
    forward(0)

    pl.semaphore_wait(far_ready, 1)

    @pl.when(inner)
    def _():
        far_sends()

    for copy in tp_copies:
        copy.wait_recv()
    packed = tp_send[...] + tp_recv[0] + tp_recv[1] + tp_recv[2]
    picked = []
    for g in range(8):
        own_adapter = adapter_ref[0, g // 4]
        rows = spread(jnp.where(lane // ADAPTER_RANK == g, packed, 0.0))
        picked.append(jnp.where(lane // ADAPTER_RANK == own_adapter, rows, 0.0))
    picked = jnp.concatenate(picked, axis=0).astype(jnp.bfloat16)
    loads[2].wait()
    loads[3].wait()
    for n in range(8):
        at = slice(n * 256, (n + 1) * 256)
        raised = jnp.dot(picked, up_v[:, at], preferred_element_type=jnp.float32)
        qfull[:, at] = (
            queries_v[:, at].astype(jnp.float32) + ADAPTER_SCALE * raised
        ).astype(jnp.bfloat16)
    own_half = pl.ds(pl.multiple_of(c * COLS, COLS), COLS)
    sib_half = pl.ds(pl.multiple_of(oc * COLS, COLS), COLS)
    query_copy = remote(
        qfull.at[:, sib_half], qx.at[c], sib_ssem.at[2], sib_rsem.at[2], sibling
    )
    query_copy.start()
    qx[c] = qfull[:, own_half]

    for j in range(1, GROUP):
        tile_wait(j, 0)
        tile_wait(j, 1)
        forward(j)
    for j in range(2):
        relay(j)

    for index, dst in ((0, sx.at[oc]), (1, len_tile.at[oc]), (2, qx.at[oc])):
        remote(dst, dst, sib_ssem.at[index], sib_rsem.at[index], sibling).wait_recv()
    own_suffix.wait()

    for g in range(8):
        rows = qx[:, :, g * 128 : (g + 1) * 128].reshape(128, 128)
        qt[:, g * 128 : (g + 1) * 128] = rows.T

    lengths = jnp.where(lane // 64 == 0, len_tile[0], len_tile[1])[0:1].astype(jnp.int32)
    key_at = lax.broadcasted_iota(jnp.int32, (128, 128), 0)
    col_at = lax.broadcasted_iota(jnp.int32, (128, 128), 1)
    limit = jnp.minimum(col_at % 32, lengths - 1)
    seen = (key_at // 32 == col_at // 32) & (key_at % 32 <= limit)
    keys = sx[:, :, :, 0:128].reshape(128, 128)
    values_t = sx[:, :, :, 128:256].reshape(128, 128).T
    for g in range(8):
        at = slice(g * 128, (g + 1) * 128)
        scores = jnp.dot(keys, qt[:, at], preferred_element_type=jnp.float32)
        scores = jnp.where(seen, scores, NEG_BIG)
        top = scores.max(axis=0, keepdims=True)
        weights = jnp.where(seen, jnp.exp2((scores - top) * EXP2_SCALE), 0.0)
        peak[:, at] = top
        total[:, at] = weights.sum(axis=0, keepdims=True)
        acc[:, at] = jnp.dot(
            values_t, weights.astype(jnp.bfloat16), preferred_element_type=jnp.float32
        )

    def attend(r, g):
        tile = kv.at[r, pl.ds(g * GROUP, GROUP)]
        keys = tile[:, :, :, 0:128].reshape(KEYS, 128)
        values_t = tile[:, :, :, 128:256].reshape(KEYS, 128).T
        from_y = (y + jnp.where(r == 0, 0, jnp.where(r == 1, 3, jnp.where(r == 2, 1, 2)))) % NY
        bias = []
        for i in range(GROUP * 4):
            held = blocks_ref[0, from_y * 4 + i % 4]
            live = source_of[g * GROUP + i // 4] < 2 * held
            bias.append(jnp.where(live, 0.0, NEG_BIG))
        for b in range(COLS // BLOCK):
            at = slice(b * BLOCK, (b + 1) * BLOCK)
            scores = jnp.dot(keys, qt[:, at], preferred_element_type=jnp.float32)
            before = peak[:, at]
            top = None
            for i in range(GROUP * 4):
                low, high = scores[16 * i : 16 * i + 8], scores[16 * i + 8 : 16 * i + 16]
                part = jnp.maximum(low, high) + bias[i]
                top = part if top is None else jnp.maximum(top, part)
            top = jnp.maximum(before, top.max(axis=0, keepdims=True))
            shrink = jnp.exp2((before - top) * EXP2_SCALE)
            scaled_top = top * EXP2_SCALE
            parts = []
            added = jnp.zeros((8, BLOCK), jnp.float32)
            for i in range(GROUP * 4):
                part = jnp.exp2(scores[16 * i : 16 * i + 16] * EXP2_SCALE - (scaled_top - bias[i]))
                added = added + (part[:8] + part[8:])
                parts.append(part.astype(jnp.bfloat16))
            peak[:, at] = top
            total[:, at] = total[:, at] * shrink + added.sum(axis=0, keepdims=True)
            acc[:, at] = acc[:, at] * shrink + jnp.dot(
                values_t, jnp.concatenate(parts, axis=0), preferred_element_type=jnp.float32
            )

    def step(k, _):
        @pl.when(k < SLOTS)
        def _():
            tile_wait(k, 0)
            tile_wait(k, 1)
            forward(k)

        @pl.when((k >= FIRST_FAR) & (k < SLOTS))
        def _():
            y_across(k).start()

        @pl.when((k == LATE) & jnp.logical_not(inner))
        def _():
            far_sends()

        @pl.when(k < FIRST_FAR + 2)
        def _():
            relay(k - 2)

        unit = k - GROUP
        g, r = unit // 4, unit % 4
        for i in range(GROUP):
            j = g * GROUP + i

            @pl.when((r == 2 - i % 2) | ((r > 0) & (j >= FIRST_FAR)) | (r == 3))
            def _():
                way = r - 1
                y_wait(way, j)

        attend(r, g)
        return 0

    lax.fori_loop(GROUP, SLOTS + GROUP, step, 0)

    keep = lax.broadcasted_iota(jnp.int32, (1, 128), 1) % 32 < lengths
    out_copies = []
    for n in range(4):
        for g in (2 * n, 2 * n + 1):
            at = slice(g * 128, (g + 1) * 128)
            rows = jnp.where(keep, acc[:, at] * (1.0 / total[:, at]), 0.0)
            rows = rows.astype(jnp.bfloat16).T
            res[:, :, at] = rows.reshape(2, 64, 128)
        half = pl.ds(pl.multiple_of(c * COLS + n * 256, 256), 256)
        copy = remote(
            res.at[oc, :, n * 256 : (n + 1) * 256],
            out.at[:, half],
            out_ssem.at[n],
            out_rsem.at[n],
            sibling,
        )
        copy.start()
        out_copies.append(copy)
    out[:, own_half] = res[c]

    def drain(j, _):
        for core in (0, 1):

            @pl.when((j > 0) | (core == oc))
            def _():
                src = kv.at[0, j, pl.ds(2 * core, 2)]
                remote(src, src, a2a_send.at[j, core], a2a_recv.at[j, core], sibling).wait_send()

        for way in (0, 1, 2):
            src = kv.at[1 + way, j]
            remote(src, src, y_send.at[way, j], y_recv.at[way, j], sibling).wait_send()
        return 0

    lax.fori_loop(0, SLOTS, drain, 0)
    for copy in tp_copies + [suffix_copy, len_copy, query_copy]:
        copy.wait_send()
    for n, copy in enumerate(out_copies):
        copy.wait_send()
        arrived = out.at[:, pl.ds(pl.multiple_of(oc * COLS + n * 256, 256), 256)]
        remote(arrived, arrived, out_ssem.at[n], out_rsem.at[n], sibling).wait_recv()


def per_device(
    visual_key_value,
    patch_blocks,
    queries,
    suffix_key_value,
    suffix_hidden_state,
    down_weight,
    up_weight,
    question_adapter,
    suffix_token_length,
):
    bf16, f32 = jnp.bfloat16, jnp.float32
    asked, positions, width = queries.shape[1:]
    rows = asked * positions
    dma = pltpu.SemaphoreType.DMA
    hbm = pl.BlockSpec(memory_space=pl.ANY)
    result = pl.pallas_call(
        kernel,
        name="attention",
        out_shape=jax.ShapeDtypeStruct((rows, width), bf16),
        in_specs=[hbm] * 9,
        out_specs=pl.BlockSpec(memory_space=pltpu.VMEM),
        scratch_shapes=[
            pltpu.VMEM((4, SLOTS, 4, 16, 256), bf16),
            pltpu.VMEM((2, 2, 32, 256), bf16),
            pltpu.VMEM((2, rows, COLS), bf16),
            pltpu.VMEM((rows, width), bf16),
            pltpu.VMEM((HEAD_SIZE, COLS), bf16),
            pltpu.VMEM((HEAD_SIZE, COLS), f32),
            pltpu.VMEM((1, COLS), f32),
            pltpu.VMEM((1, COLS), f32),
            pltpu.VMEM((2, rows, COLS), bf16),
            pltpu.VMEM((rows, width), bf16),
            pltpu.VMEM(down_weight.shape, bf16),
            pltpu.VMEM(up_weight.shape, bf16),
            pltpu.VMEM((rows, width), bf16),
            pltpu.VMEM((8, 128), f32),
            pltpu.VMEM((3, 8, 128), f32),
            pltpu.VMEM((2, 8, 128), f32),
            pltpu.SMEM((SLOTS,), jnp.int32),
            pltpu.SMEM(patch_blocks.shape, jnp.int32),
            pltpu.SMEM(question_adapter.shape, jnp.int32),
            pltpu.SMEM(suffix_token_length.shape, jnp.int32),
            dma((9,)),
            dma((SLOTS, 2)),
            dma((SLOTS, 2)),
            dma((3, SLOTS)),
            dma((3, SLOTS)),
            dma((3,)),
            dma((3,)),
            dma((3,)),
            dma((3,)),
            dma((4,)),
            dma((4,)),
            pltpu.SemaphoreType.REGULAR,
        ],
        compiler_params=pltpu.CompilerParams(
            collective_id=0, has_side_effects=True, vmem_limit_bytes=56 << 20
        ),
    )(
        patch_blocks,
        question_adapter,
        suffix_token_length,
        visual_key_value,
        queries.reshape(rows, width),
        suffix_key_value.reshape(asked, positions, -1),
        suffix_hidden_state.reshape(rows, width),
        down_weight,
        up_weight,
    )
    return result.reshape(queries.shape)


def solution(mesh):
    placed = (
        P(None, "seq", "enc", "tp"),
        P("enc", None),
        P("enc", "seq", None, "tp"),
        P("enc", "seq", None, "tp"),
        P("enc", "seq", None, "tp"),
        P("tp", None),
        P(None, "tp"),
        P("enc", "seq"),
        P("enc", "seq"),
    )
    return jax.shard_map(
        per_device,
        mesh=mesh,
        in_specs=placed,
        out_specs=P("enc", "seq", None, "tp"),
        check_vma=False,
    )
```

```python
import math

import jax
import jax.numpy as jnp
from jax import lax
from jax.experimental import pallas as pl
from jax.experimental.pallas import tpu as pltpu
from jax.sharding import PartitionSpec as P

MESH = pl.DeviceIdType.MESH
HEAD_SIZE = 128
ADAPTER_RANK = 16
ADAPTER_SCALE = 2.0
NEG_BIG = -1e30
NX, NZ, NY = 4, 4, 4
SLOTS = NX * NZ
GROUP = 4
KEYS = GROUP * 64
COLS = 1024
BLOCK = 128
EXP2_SCALE = math.log2(math.e) / math.sqrt(HEAD_SIZE)
HERE = [(0, 0), (1, 0), (3, 0), (2, 0)]
NEAR = [(dx, dz) for dx in (2, 3, 1, 0) for dz in (1, 3)]
FAR = [(dx, 2) for dx in (2, 3, 1, 0)]
OFFSETS = HERE + NEAR + FAR
FIRST_FAR = len(HERE + NEAR)
LATE = GROUP + 1
HELD = SLOTS - 2


def spread(rows):
    for shift in (64, 32, 16):
        rows = rows + pltpu.roll(rows, shift, 1)
    return rows


def kernel(
    blocks,
    adapter,
    length,
    visual,
    queries,
    suffix,
    hidden,
    down,
    up,
    out,
    kv,
    sx,
    qx,
    qfull,
    qt,
    acc,
    peak,
    total,
    res,
    hidden_v,
    down_v,
    up_v,
    queries_v,
    tp_send,
    tp_recv,
    len_tile,
    source_of,
    blocks_ref,
    adapter_ref,
    length_ref,
    load_sem,
    a2a_send,
    a2a_recv,
    y_send,
    y_recv,
    tp_ssem,
    tp_rsem,
    sib_ssem,
    sib_rsem,
    out_ssem,
    out_rsem,
    far_ready,
    pair_ready,
):
    e, s, t = lax.axis_index("enc"), lax.axis_index("seq"), lax.axis_index("tp")
    x, z = e // NZ, e % NZ
    y, c = s // 2, s % 2
    oc = 1 - c

    def enc_at(dx, dz):
        return ((x + dx) % NX) * NZ + (z + dz) % NZ

    def y_at(dy):
        return (e, ((y + dy) % NY) * 2 + c, t)

    sibling = (e, y * 2 + oc, t)

    barrier = pltpu.get_barrier_semaphore()
    peers = [sibling, y_at(1), y_at(2), y_at(3)]
    peers += [(e, s, (t + k) % 4) for k in (1, 2, 3)]
    for dx, dz in (HERE + NEAR)[1:]:
        peers.append((enc_at(dx, dz), s, t))
    for peer in peers:
        pl.semaphore_signal(barrier, inc=1, device_id=peer, device_id_type=MESH)

    loads = [
        pltpu.make_async_copy(src, dst, load_sem.at[i])
        for i, (src, dst) in enumerate(
            ((hidden, hidden_v), (down, down_v), (up, up_v), (queries, queries_v))
        )
    ]
    for load in loads:
        load.start()
    scalars = [
        pltpu.make_async_copy(src, dst, load_sem.at[6 + i])
        for i, (src, dst) in enumerate(
            ((blocks, blocks_ref), (adapter, adapter_ref), (length, length_ref))
        )
    ]
    for load in scalars:
        load.start()
    own_cols = pl.ds(pl.multiple_of(c * 256, 256), 256)
    sib_cols = pl.ds(pl.multiple_of(oc * 256, 256), 256)
    own_tile = pltpu.make_async_copy(
        visual.at[e, :, :, own_cols], kv.at[0, 0, pl.ds(2 * c, 2)], load_sem.at[4]
    )
    own_tile.start()
    own_suffix = pltpu.make_async_copy(
        suffix.at[:, :, own_cols], sx.at[c], load_sem.at[5]
    )
    own_suffix.start()

    for j, (dx, dz) in enumerate(OFFSETS):
        source_of[j] = enc_at(NX - dx, NZ - dz)

    lane = lax.broadcasted_iota(jnp.int32, (8, 128), 1)
    for load in [loads[0], loads[1], *scalars]:
        load.wait()
    lowered = jnp.dot(hidden_v[...], down_v[...], preferred_element_type=jnp.float32)
    packed = jnp.zeros((8, 128), jnp.float32)
    for g in range(8):
        own_adapter = adapter_ref[0, g // 4]
        rows = jnp.where(lane // ADAPTER_RANK == own_adapter, lowered[8 * g : 8 * g + 8], 0.0)
        packed = jnp.where(lane // ADAPTER_RANK == g, spread(rows), packed)
    tp_send[...] = packed
    len_tile[c] = jnp.where((lane // 32) % 2 == 0, length_ref[0, 0], length_ref[0, 1]).astype(
        jnp.float32
    )

    pl.semaphore_wait(barrier, len(peers))

    pl.semaphore_signal(pair_ready, inc=1, device_id=sibling, device_id_type=MESH)

    def remote(src, dst, ssem, rsem, device):
        return pltpu.make_async_remote_copy(
            src_ref=src,
            dst_ref=dst,
            send_sem=ssem,
            recv_sem=rsem,
            device_id=device,
            device_id_type=MESH,
        )

    tp_copies = [
        remote(
            tp_send, tp_recv.at[k - 1], tp_ssem.at[k - 1], tp_rsem.at[k - 1], (e, s, (t + k) % 4)
        )
        for k in (1, 2, 3)
    ]
    for copy in tp_copies:
        copy.start()

    def tile_send(dx, dz, j, core, cols):
        target = enc_at(dx, dz)
        return remote(
            visual.at[target, :, :, cols],
            kv.at[0, j, pl.ds(2 * c, 2)],
            a2a_send.at[j, core],
            a2a_recv.at[j, c],
            (target, y * 2 + core, t),
        )

    tile_send(0, 0, 0, oc, sib_cols).start()
    suffix_copy = remote(
        suffix.at[:, :, sib_cols], sx.at[c], sib_ssem.at[0], sib_rsem.at[0], sibling
    )
    suffix_copy.start()
    len_copy = remote(len_tile.at[c], len_tile.at[c], sib_ssem.at[1], sib_rsem.at[1], sibling)
    len_copy.start()
    for j in range(1, GROUP + 2):
        tile_send(*OFFSETS[j], j, c, own_cols).start()
    pl.semaphore_wait(pair_ready, 1)
    for j in range(1, GROUP + 2):
        tile_send(*OFFSETS[j], j, oc, sib_cols).start()
    for j in range(GROUP + 2, FIRST_FAR):
        tile_send(*OFFSETS[j], j, c, own_cols).start()
        tile_send(*OFFSETS[j], j, oc, sib_cols).start()
    pl.semaphore_signal(
        far_ready, inc=1, device_id=(enc_at(0, NZ - 1), s, t), device_id_type=MESH
    )

    def far_sends():
        for j in range(FIRST_FAR, SLOTS):
            tile_send(*OFFSETS[j], j, c, own_cols).start()
            tile_send(*OFFSETS[j], j, oc, sib_cols).start()

    inner = (t == 1) | (t == 2)

    def tile_wait(j, core):
        dst = kv.at[0, j, pl.ds(2 * core, 2)]
        remote(dst, dst, a2a_send.at[j, core], a2a_recv.at[j, core], sibling).wait_recv()

    def y_copy(way, j):
        return remote(
            kv.at[0, j],
            kv.at[1 + way, j],
            y_send.at[way, j],
            y_recv.at[way, j],
            y_at(1 if way == 0 else 3),
        )

    def y_relay(j):
        way = j % 2
        return remote(
            kv.at[1 + way, j],
            kv.at[3, j],
            y_send.at[2, j],
            y_recv.at[2, j],
            (e, ((y + 1 + 2 * way) % NY) * 2 + c, t),
        )

    def y_across(j):
        return remote(
            kv.at[0, j], kv.at[3, j], y_send.at[2, j], y_recv.at[2, j], y_at(2)
        )

    def y_wait(way, j):
        dst = kv.at[1 + way, j]
        remote(dst, dst, y_send.at[way, j], y_recv.at[way, j], sibling).wait_recv()

    def forward(j):
        y_copy(0, j).start()
        y_copy(1, j).start()

    def relay(j):
        y_wait(j % 2, j)
        y_relay(j).start()

    own_tile.wait()
    tile_wait(0, oc)
    forward(0)

    pl.semaphore_wait(far_ready, 1)

    @pl.when(inner)
    def _():
        far_sends()

    for copy in tp_copies:
        copy.wait_recv()
    packed = tp_send[...] + tp_recv[0] + tp_recv[1] + tp_recv[2]
    picked = []
    for g in range(8):
        own_adapter = adapter_ref[0, g // 4]
        rows = spread(jnp.where(lane // ADAPTER_RANK == g, packed, 0.0))
        picked.append(jnp.where(lane // ADAPTER_RANK == own_adapter, rows, 0.0))
    picked = jnp.concatenate(picked, axis=0).astype(jnp.bfloat16)
    loads[2].wait()
    loads[3].wait()
    for n in range(8):
        at = slice(n * 256, (n + 1) * 256)
        raised = jnp.dot(picked, up_v[:, at], preferred_element_type=jnp.float32)
        qfull[:, at] = (
            queries_v[:, at].astype(jnp.float32) + ADAPTER_SCALE * raised
        ).astype(jnp.bfloat16)
    own_half = pl.ds(pl.multiple_of(c * COLS, COLS), COLS)
    sib_half = pl.ds(pl.multiple_of(oc * COLS, COLS), COLS)
    query_copy = remote(
        qfull.at[:, sib_half], qx.at[c], sib_ssem.at[2], sib_rsem.at[2], sibling
    )
    query_copy.start()
    qx[c] = qfull[:, own_half]

    for j in range(1, GROUP):
        tile_wait(j, 0)
        tile_wait(j, 1)
        forward(j)
    for j in range(2):
        relay(j)

    for index, dst in ((0, sx.at[oc]), (1, len_tile.at[oc]), (2, qx.at[oc])):
        remote(dst, dst, sib_ssem.at[index], sib_rsem.at[index], sibling).wait_recv()
    own_suffix.wait()

    for g in range(8):
        rows = qx[:, :, g * 128 : (g + 1) * 128].reshape(128, 128)
        qt[:, g * 128 : (g + 1) * 128] = rows.T

    lengths = jnp.where(lane // 64 == 0, len_tile[0], len_tile[1])[0:1].astype(jnp.int32)
    key_at = lax.broadcasted_iota(jnp.int32, (128, 128), 0)
    col_at = lax.broadcasted_iota(jnp.int32, (128, 128), 1)
    limit = jnp.minimum(col_at % 32, lengths - 1)
    seen = (key_at // 32 == col_at // 32) & (key_at % 32 <= limit)
    keys = sx[:, :, :, 0:128].reshape(128, 128)
    values_t = sx[:, :, :, 128:256].reshape(128, 128).T
    for g in range(8):
        at = slice(g * 128, (g + 1) * 128)
        scores = jnp.dot(keys, qt[:, at], preferred_element_type=jnp.float32)
        scores = jnp.where(seen, scores, NEG_BIG)
        top = scores.max(axis=0, keepdims=True)
        weights = jnp.where(seen, jnp.exp2((scores - top) * EXP2_SCALE), 0.0)
        peak[:, at] = top
        total[:, at] = weights.sum(axis=0, keepdims=True)
        acc[:, at] = jnp.dot(
            values_t, weights.astype(jnp.bfloat16), preferred_element_type=jnp.float32
        )

    def attend(r, g):
        tile = kv.at[r, pl.ds(g * GROUP, GROUP)]
        keys = tile[:, :, :, 0:128].reshape(KEYS, 128)
        values_t = tile[:, :, :, 128:256].reshape(KEYS, 128).T
        from_y = (y + jnp.where(r == 0, 0, jnp.where(r == 1, 3, jnp.where(r == 2, 1, 2)))) % NY
        bias = []
        for i in range(GROUP * 4):
            held = blocks_ref[0, from_y * 4 + i % 4]
            live = source_of[g * GROUP + i // 4] < 2 * held
            bias.append(jnp.where(live, 0.0, NEG_BIG))
        for b in range(COLS // BLOCK):
            at = slice(b * BLOCK, (b + 1) * BLOCK)
            scores = jnp.dot(keys, qt[:, at], preferred_element_type=jnp.float32)
            before = peak[:, at]
            top = None
            for i in range(GROUP * 4):
                low, high = scores[16 * i : 16 * i + 8], scores[16 * i + 8 : 16 * i + 16]
                part = jnp.maximum(low, high) + bias[i]
                top = part if top is None else jnp.maximum(top, part)
            top = jnp.maximum(before, top.max(axis=0, keepdims=True))
            shrink = jnp.exp2((before - top) * EXP2_SCALE)
            scaled_top = top * EXP2_SCALE
            parts = []
            added = jnp.zeros((8, BLOCK), jnp.float32)
            for i in range(GROUP * 4):
                part = jnp.exp2(scores[16 * i : 16 * i + 16] * EXP2_SCALE - (scaled_top - bias[i]))
                added = added + (part[:8] + part[8:])
                parts.append(part.astype(jnp.bfloat16))
            peak[:, at] = top
            total[:, at] = total[:, at] * shrink + added.sum(axis=0, keepdims=True)
            acc[:, at] = acc[:, at] * shrink + jnp.dot(
                values_t, jnp.concatenate(parts, axis=0), preferred_element_type=jnp.float32
            )

    def step(k, _):
        @pl.when(k < SLOTS)
        def _():
            tile_wait(k, 0)
            tile_wait(k, 1)
            forward(k)

        @pl.when((k >= FIRST_FAR) & (k < SLOTS))
        def _():
            y_across(k).start()

        @pl.when((k == LATE) & jnp.logical_not(inner))
        def _():
            far_sends()

        @pl.when(k < FIRST_FAR + 2)
        def _():
            relay(k - 2)

        @pl.when((k < HELD) | (k >= SLOTS))
        def _():
            unit = jnp.where(k < SLOTS, k - GROUP, k - GROUP - (SLOTS - HELD))
            g, r = unit // 4, unit % 4
            for i in range(GROUP):
                j = g * GROUP + i

                @pl.when((r == 2 - i % 2) | ((r > 0) & (j >= FIRST_FAR)) | (r == 3))
                def _():
                    y_wait(r - 1, j)

            attend(r, g)

        return 0

    lax.fori_loop(GROUP, SLOTS + GROUP + (SLOTS - HELD), step, 0)

    keep = lax.broadcasted_iota(jnp.int32, (1, 128), 1) % 32 < lengths
    out_copies = []
    for n in range(4):
        for g in (2 * n, 2 * n + 1):
            at = slice(g * 128, (g + 1) * 128)
            rows = jnp.where(keep, acc[:, at] * (1.0 / total[:, at]), 0.0)
            rows = rows.astype(jnp.bfloat16).T
            res[:, :, at] = rows.reshape(2, 64, 128)
        half = pl.ds(pl.multiple_of(c * COLS + n * 256, 256), 256)
        copy = remote(
            res.at[oc, :, n * 256 : (n + 1) * 256],
            out.at[:, half],
            out_ssem.at[n],
            out_rsem.at[n],
            sibling,
        )
        copy.start()
        out_copies.append(copy)
    out[:, own_half] = res[c]

    def drain(j, _):
        for core in (0, 1):

            @pl.when((j > 0) | (core == oc))
            def _():
                src = kv.at[0, j, pl.ds(2 * core, 2)]
                remote(src, src, a2a_send.at[j, core], a2a_recv.at[j, core], sibling).wait_send()

        for way in (0, 1, 2):
            src = kv.at[1 + way, j]
            remote(src, src, y_send.at[way, j], y_recv.at[way, j], sibling).wait_send()
        return 0

    lax.fori_loop(0, SLOTS, drain, 0)
    for copy in tp_copies + [suffix_copy, len_copy, query_copy]:
        copy.wait_send()
    for n, copy in enumerate(out_copies):
        copy.wait_send()
        arrived = out.at[:, pl.ds(pl.multiple_of(oc * COLS + n * 256, 256), 256)]
        remote(arrived, arrived, out_ssem.at[n], out_rsem.at[n], sibling).wait_recv()


def per_device(
    visual_key_value,
    patch_blocks,
    queries,
    suffix_key_value,
    suffix_hidden_state,
    down_weight,
    up_weight,
    question_adapter,
    suffix_token_length,
):
    bf16, f32 = jnp.bfloat16, jnp.float32
    asked, positions, width = queries.shape[1:]
    rows = asked * positions
    dma = pltpu.SemaphoreType.DMA
    hbm = pl.BlockSpec(memory_space=pl.ANY)
    result = pl.pallas_call(
        kernel,
        name="attention",
        out_shape=jax.ShapeDtypeStruct((rows, width), bf16),
        in_specs=[hbm] * 9,
        out_specs=pl.BlockSpec(memory_space=pltpu.VMEM),
        scratch_shapes=[
            pltpu.VMEM((4, SLOTS, 4, 16, 256), bf16),
            pltpu.VMEM((2, 2, 32, 256), bf16),
            pltpu.VMEM((2, rows, COLS), bf16),
            pltpu.VMEM((rows, width), bf16),
            pltpu.VMEM((HEAD_SIZE, COLS), bf16),
            pltpu.VMEM((HEAD_SIZE, COLS), f32),
            pltpu.VMEM((1, COLS), f32),
            pltpu.VMEM((1, COLS), f32),
            pltpu.VMEM((2, rows, COLS), bf16),
            pltpu.VMEM((rows, width), bf16),
            pltpu.VMEM(down_weight.shape, bf16),
            pltpu.VMEM(up_weight.shape, bf16),
            pltpu.VMEM((rows, width), bf16),
            pltpu.VMEM((8, 128), f32),
            pltpu.VMEM((3, 8, 128), f32),
            pltpu.VMEM((2, 8, 128), f32),
            pltpu.SMEM((SLOTS,), jnp.int32),
            pltpu.SMEM(patch_blocks.shape, jnp.int32),
            pltpu.SMEM(question_adapter.shape, jnp.int32),
            pltpu.SMEM(suffix_token_length.shape, jnp.int32),
            dma((9,)),
            dma((SLOTS, 2)),
            dma((SLOTS, 2)),
            dma((3, SLOTS)),
            dma((3, SLOTS)),
            dma((3,)),
            dma((3,)),
            dma((3,)),
            dma((3,)),
            dma((4,)),
            dma((4,)),
            pltpu.SemaphoreType.REGULAR,
            pltpu.SemaphoreType.REGULAR,
        ],
        compiler_params=pltpu.CompilerParams(
            collective_id=0, has_side_effects=True, vmem_limit_bytes=56 << 20
        ),
    )(
        patch_blocks,
        question_adapter,
        suffix_token_length,
        visual_key_value,
        queries.reshape(rows, width),
        suffix_key_value.reshape(asked, positions, -1),
        suffix_hidden_state.reshape(rows, width),
        down_weight,
        up_weight,
    )
    return result.reshape(queries.shape)


def solution(mesh):
    placed = (
        P(None, "seq", "enc", "tp"),
        P("enc", None),
        P("enc", "seq", None, "tp"),
        P("enc", "seq", None, "tp"),
        P("enc", "seq", None, "tp"),
        P("tp", None),
        P(None, "tp"),
        P("enc", "seq"),
        P("enc", "seq"),
    )
    return jax.shard_map(
        per_device,
        mesh=mesh,
        in_specs=placed,
        out_specs=P("enc", "seq", None, "tp"),
        check_vma=False,
    )
```

```python
import math

import jax
import jax.numpy as jnp
from jax import lax
from jax.experimental import pallas as pl
from jax.experimental.pallas import tpu as pltpu
from jax.sharding import PartitionSpec as P

MESH = pl.DeviceIdType.MESH
HEAD_SIZE = 128
ADAPTER_RANK = 16
ADAPTER_SCALE = 2.0
NEG_BIG = -1e30
NX, NZ, NY = 4, 4, 4
SLOTS = NX * NZ
GROUP = 4
KEYS = GROUP * 64
COLS = 1024
BLOCK = 128
EXP2_SCALE = math.log2(math.e) / math.sqrt(HEAD_SIZE)
HERE = [(0, 0), (1, 0), (3, 0), (2, 0)]
NEAR = [(dx, dz) for dx in (0, 1, 3, 2) for dz in (1, 3)]
FAR = [(dx, 2) for dx in (2, 3, 1, 0)]
OFFSETS = HERE + NEAR + FAR
FIRST_FAR = len(HERE + NEAR)
LATE = GROUP + 1
HELD = SLOTS - 2


def spread(rows):
    for shift in (64, 32, 16):
        rows = rows + pltpu.roll(rows, shift, 1)
    return rows


def kernel(
    blocks,
    adapter,
    length,
    visual,
    queries,
    suffix,
    hidden,
    down,
    up,
    out,
    kv,
    sx,
    qx,
    qfull,
    qt,
    acc,
    peak,
    total,
    res,
    hidden_v,
    down_v,
    up_v,
    queries_v,
    tp_send,
    tp_recv,
    len_tile,
    source_of,
    blocks_ref,
    adapter_ref,
    length_ref,
    load_sem,
    a2a_send,
    a2a_recv,
    y_send,
    y_recv,
    tp_ssem,
    tp_rsem,
    sib_ssem,
    sib_rsem,
    out_ssem,
    out_rsem,
    far_ready,
    pair_ready,
):
    e, s, t = lax.axis_index("enc"), lax.axis_index("seq"), lax.axis_index("tp")
    x, z = e // NZ, e % NZ
    y, c = s // 2, s % 2
    oc = 1 - c

    def enc_at(dx, dz):
        return ((x + dx) % NX) * NZ + (z + dz) % NZ

    def y_at(dy):
        return (e, ((y + dy) % NY) * 2 + c, t)

    sibling = (e, y * 2 + oc, t)

    barrier = pltpu.get_barrier_semaphore()
    peers = [sibling, y_at(1), y_at(2), y_at(3)]
    peers += [(e, s, (t + k) % 4) for k in (1, 2, 3)]
    for dx, dz in (HERE + NEAR)[1:]:
        peers.append((enc_at(dx, dz), s, t))
    for peer in peers:
        pl.semaphore_signal(barrier, inc=1, device_id=peer, device_id_type=MESH)

    loads = [
        pltpu.make_async_copy(src, dst, load_sem.at[i])
        for i, (src, dst) in enumerate(
            ((hidden, hidden_v), (down, down_v), (up, up_v), (queries, queries_v))
        )
    ]
    for load in loads:
        load.start()
    scalars = [
        pltpu.make_async_copy(src, dst, load_sem.at[6 + i])
        for i, (src, dst) in enumerate(
            ((blocks, blocks_ref), (adapter, adapter_ref), (length, length_ref))
        )
    ]
    for load in scalars:
        load.start()
    own_cols = pl.ds(pl.multiple_of(c * 256, 256), 256)
    sib_cols = pl.ds(pl.multiple_of(oc * 256, 256), 256)
    own_tile = pltpu.make_async_copy(
        visual.at[e, :, :, own_cols], kv.at[0, 0, pl.ds(2 * c, 2)], load_sem.at[4]
    )
    own_tile.start()
    own_suffix = pltpu.make_async_copy(
        suffix.at[:, :, own_cols], sx.at[c], load_sem.at[5]
    )
    own_suffix.start()

    for j, (dx, dz) in enumerate(OFFSETS):
        source_of[j] = enc_at(NX - dx, NZ - dz)

    lane = lax.broadcasted_iota(jnp.int32, (8, 128), 1)
    for load in [loads[0], loads[1], *scalars]:
        load.wait()
    lowered = jnp.dot(hidden_v[...], down_v[...], preferred_element_type=jnp.float32)
    packed = jnp.zeros((8, 128), jnp.float32)
    for g in range(8):
        own_adapter = adapter_ref[0, g // 4]
        rows = jnp.where(lane // ADAPTER_RANK == own_adapter, lowered[8 * g : 8 * g + 8], 0.0)
        packed = jnp.where(lane // ADAPTER_RANK == g, spread(rows), packed)
    tp_send[...] = packed
    len_tile[c] = jnp.where((lane // 32) % 2 == 0, length_ref[0, 0], length_ref[0, 1]).astype(
        jnp.float32
    )

    pl.semaphore_wait(barrier, len(peers))

    pl.semaphore_signal(pair_ready, inc=1, device_id=sibling, device_id_type=MESH)

    def remote(src, dst, ssem, rsem, device):
        return pltpu.make_async_remote_copy(
            src_ref=src,
            dst_ref=dst,
            send_sem=ssem,
            recv_sem=rsem,
            device_id=device,
            device_id_type=MESH,
        )

    tp_copies = [
        remote(
            tp_send, tp_recv.at[k - 1], tp_ssem.at[k - 1], tp_rsem.at[k - 1], (e, s, (t + k) % 4)
        )
        for k in (1, 2, 3)
    ]
    for copy in tp_copies:
        copy.start()

    def tile_send(dx, dz, j, core, cols):
        target = enc_at(dx, dz)
        return remote(
            visual.at[target, :, :, cols],
            kv.at[0, j, pl.ds(2 * c, 2)],
            a2a_send.at[j, core],
            a2a_recv.at[j, c],
            (target, y * 2 + core, t),
        )

    tile_send(0, 0, 0, oc, sib_cols).start()
    suffix_copy = remote(
        suffix.at[:, :, sib_cols], sx.at[c], sib_ssem.at[0], sib_rsem.at[0], sibling
    )
    suffix_copy.start()
    len_copy = remote(len_tile.at[c], len_tile.at[c], sib_ssem.at[1], sib_rsem.at[1], sibling)
    len_copy.start()
    for j in range(1, GROUP + 2):
        tile_send(*OFFSETS[j], j, c, own_cols).start()
    pl.semaphore_wait(pair_ready, 1)
    for j in range(1, GROUP + 2):
        tile_send(*OFFSETS[j], j, oc, sib_cols).start()
    for j in range(GROUP + 2, FIRST_FAR):
        tile_send(*OFFSETS[j], j, c, own_cols).start()
        tile_send(*OFFSETS[j], j, oc, sib_cols).start()
    pl.semaphore_signal(
        far_ready, inc=1, device_id=(enc_at(0, NZ - 1), s, t), device_id_type=MESH
    )

    def far_sends():
        for j in range(FIRST_FAR, SLOTS):
            tile_send(*OFFSETS[j], j, c, own_cols).start()
            tile_send(*OFFSETS[j], j, oc, sib_cols).start()

    inner = (t == 1) | (t == 2)

    def tile_wait(j, core):
        dst = kv.at[0, j, pl.ds(2 * core, 2)]
        remote(dst, dst, a2a_send.at[j, core], a2a_recv.at[j, core], sibling).wait_recv()

    def y_copy(way, j):
        return remote(
            kv.at[0, j],
            kv.at[1 + way, j],
            y_send.at[way, j],
            y_recv.at[way, j],
            y_at(1 if way == 0 else 3),
        )

    def y_relay(j):
        way = j % 2
        return remote(
            kv.at[1 + way, j],
            kv.at[3, j],
            y_send.at[2, j],
            y_recv.at[2, j],
            (e, ((y + 1 + 2 * way) % NY) * 2 + c, t),
        )

    def y_across(j):
        return remote(
            kv.at[0, j], kv.at[3, j], y_send.at[2, j], y_recv.at[2, j], y_at(2)
        )

    def y_wait(way, j):
        dst = kv.at[1 + way, j]
        remote(dst, dst, y_send.at[way, j], y_recv.at[way, j], sibling).wait_recv()

    def forward(j):
        y_copy(0, j).start()
        y_copy(1, j).start()

    def relay(j):
        y_wait(j % 2, j)
        y_relay(j).start()

    own_tile.wait()
    tile_wait(0, oc)
    forward(0)

    pl.semaphore_wait(far_ready, 1)

    @pl.when(inner)
    def _():
        far_sends()

    for copy in tp_copies:
        copy.wait_recv()
    packed = tp_send[...] + tp_recv[0] + tp_recv[1] + tp_recv[2]
    picked = []
    for g in range(8):
        own_adapter = adapter_ref[0, g // 4]
        rows = spread(jnp.where(lane // ADAPTER_RANK == g, packed, 0.0))
        picked.append(jnp.where(lane // ADAPTER_RANK == own_adapter, rows, 0.0))
    picked = jnp.concatenate(picked, axis=0).astype(jnp.bfloat16)
    loads[2].wait()
    loads[3].wait()
    for n in range(8):
        at = slice(n * 256, (n + 1) * 256)
        raised = jnp.dot(picked, up_v[:, at], preferred_element_type=jnp.float32)
        qfull[:, at] = (
            queries_v[:, at].astype(jnp.float32) + ADAPTER_SCALE * raised
        ).astype(jnp.bfloat16)
    own_half = pl.ds(pl.multiple_of(c * COLS, COLS), COLS)
    sib_half = pl.ds(pl.multiple_of(oc * COLS, COLS), COLS)
    query_copy = remote(
        qfull.at[:, sib_half], qx.at[c], sib_ssem.at[2], sib_rsem.at[2], sibling
    )
    query_copy.start()
    qx[c] = qfull[:, own_half]

    for j in range(1, GROUP):
        tile_wait(j, 0)
        tile_wait(j, 1)
        forward(j)
    for j in range(2):
        relay(j)

    for index, dst in ((0, sx.at[oc]), (1, len_tile.at[oc]), (2, qx.at[oc])):
        remote(dst, dst, sib_ssem.at[index], sib_rsem.at[index], sibling).wait_recv()
    own_suffix.wait()

    for g in range(8):
        rows = qx[:, :, g * 128 : (g + 1) * 128].reshape(128, 128)
        qt[:, g * 128 : (g + 1) * 128] = rows.T

    lengths = jnp.where(lane // 64 == 0, len_tile[0], len_tile[1])[0:1].astype(jnp.int32)
    key_at = lax.broadcasted_iota(jnp.int32, (128, 128), 0)
    col_at = lax.broadcasted_iota(jnp.int32, (128, 128), 1)
    limit = jnp.minimum(col_at % 32, lengths - 1)
    seen = (key_at // 32 == col_at // 32) & (key_at % 32 <= limit)
    keys = sx[:, :, :, 0:128].reshape(128, 128)
    values_t = sx[:, :, :, 128:256].reshape(128, 128).T
    for g in range(8):
        at = slice(g * 128, (g + 1) * 128)
        scores = jnp.dot(keys, qt[:, at], preferred_element_type=jnp.float32)
        scores = jnp.where(seen, scores, NEG_BIG)
        top = scores.max(axis=0, keepdims=True)
        weights = jnp.where(seen, jnp.exp2((scores - top) * EXP2_SCALE), 0.0)
        peak[:, at] = top
        total[:, at] = weights.sum(axis=0, keepdims=True)
        acc[:, at] = jnp.dot(
            values_t, weights.astype(jnp.bfloat16), preferred_element_type=jnp.float32
        )

    def attend(r, g):
        tile = kv.at[r, pl.ds(g * GROUP, GROUP)]
        keys = tile[:, :, :, 0:128].reshape(KEYS, 128)
        values_t = tile[:, :, :, 128:256].reshape(KEYS, 128).T
        from_y = (y + jnp.where(r == 0, 0, jnp.where(r == 1, 3, jnp.where(r == 2, 1, 2)))) % NY
        bias = []
        for i in range(GROUP * 4):
            held = blocks_ref[0, from_y * 4 + i % 4]
            live = source_of[g * GROUP + i // 4] < 2 * held
            bias.append(jnp.where(live, 0.0, NEG_BIG))
        for b in range(COLS // BLOCK):
            at = slice(b * BLOCK, (b + 1) * BLOCK)
            scores = jnp.dot(keys, qt[:, at], preferred_element_type=jnp.float32)
            before = peak[:, at]
            top = None
            for i in range(GROUP * 4):
                low, high = scores[16 * i : 16 * i + 8], scores[16 * i + 8 : 16 * i + 16]
                part = jnp.maximum(low, high) + bias[i]
                top = part if top is None else jnp.maximum(top, part)
            top = jnp.maximum(before, top.max(axis=0, keepdims=True))
            shrink = jnp.exp2((before - top) * EXP2_SCALE)
            scaled_top = top * EXP2_SCALE
            parts = []
            added = jnp.zeros((8, BLOCK), jnp.float32)
            for i in range(GROUP * 4):
                part = jnp.exp2(scores[16 * i : 16 * i + 16] * EXP2_SCALE - (scaled_top - bias[i]))
                added = added + (part[:8] + part[8:])
                parts.append(part.astype(jnp.bfloat16))
            peak[:, at] = top
            total[:, at] = total[:, at] * shrink + added.sum(axis=0, keepdims=True)
            acc[:, at] = acc[:, at] * shrink + jnp.dot(
                values_t, jnp.concatenate(parts, axis=0), preferred_element_type=jnp.float32
            )

    def step(k, _):
        @pl.when(k < SLOTS)
        def _():
            tile_wait(k, 0)
            tile_wait(k, 1)
            forward(k)

        @pl.when((k >= FIRST_FAR) & (k < SLOTS))
        def _():
            y_across(k).start()

        @pl.when((k == LATE) & jnp.logical_not(inner))
        def _():
            far_sends()

        @pl.when(k < FIRST_FAR + 2)
        def _():
            relay(k - 2)

        @pl.when((k < HELD) | (k >= SLOTS))
        def _():
            unit = jnp.where(k < SLOTS, k - GROUP, k - GROUP - (SLOTS - HELD))
            g, r = unit // 4, unit % 4
            for i in range(GROUP):
                j = g * GROUP + i

                @pl.when((r == 2 - i % 2) | ((r > 0) & (j >= FIRST_FAR)) | (r == 3))
                def _():
                    y_wait(r - 1, j)

            attend(r, g)

        return 0

    lax.fori_loop(GROUP, SLOTS + GROUP + (SLOTS - HELD), step, 0)

    keep = lax.broadcasted_iota(jnp.int32, (1, 128), 1) % 32 < lengths
    out_copies = []
    for n in range(4):
        for g in (2 * n, 2 * n + 1):
            at = slice(g * 128, (g + 1) * 128)
            rows = jnp.where(keep, acc[:, at] * (1.0 / total[:, at]), 0.0)
            rows = rows.astype(jnp.bfloat16).T
            res[:, :, at] = rows.reshape(2, 64, 128)
        half = pl.ds(pl.multiple_of(c * COLS + n * 256, 256), 256)
        copy = remote(
            res.at[oc, :, n * 256 : (n + 1) * 256],
            out.at[:, half],
            out_ssem.at[n],
            out_rsem.at[n],
            sibling,
        )
        copy.start()
        out_copies.append(copy)
    out[:, own_half] = res[c]

    def drain(j, _):
        for core in (0, 1):

            @pl.when((j > 0) | (core == oc))
            def _():
                src = kv.at[0, j, pl.ds(2 * core, 2)]
                remote(src, src, a2a_send.at[j, core], a2a_recv.at[j, core], sibling).wait_send()

        for way in (0, 1, 2):
            src = kv.at[1 + way, j]
            remote(src, src, y_send.at[way, j], y_recv.at[way, j], sibling).wait_send()
        return 0

    lax.fori_loop(0, SLOTS, drain, 0)
    for copy in tp_copies + [suffix_copy, len_copy, query_copy]:
        copy.wait_send()
    for n, copy in enumerate(out_copies):
        copy.wait_send()
        arrived = out.at[:, pl.ds(pl.multiple_of(oc * COLS + n * 256, 256), 256)]
        remote(arrived, arrived, out_ssem.at[n], out_rsem.at[n], sibling).wait_recv()


def per_device(
    visual_key_value,
    patch_blocks,
    queries,
    suffix_key_value,
    suffix_hidden_state,
    down_weight,
    up_weight,
    question_adapter,
    suffix_token_length,
):
    bf16, f32 = jnp.bfloat16, jnp.float32
    asked, positions, width = queries.shape[1:]
    rows = asked * positions
    dma = pltpu.SemaphoreType.DMA
    hbm = pl.BlockSpec(memory_space=pl.ANY)
    result = pl.pallas_call(
        kernel,
        name="attention",
        out_shape=jax.ShapeDtypeStruct((rows, width), bf16),
        in_specs=[hbm] * 9,
        out_specs=pl.BlockSpec(memory_space=pltpu.VMEM),
        scratch_shapes=[
            pltpu.VMEM((4, SLOTS, 4, 16, 256), bf16),
            pltpu.VMEM((2, 2, 32, 256), bf16),
            pltpu.VMEM((2, rows, COLS), bf16),
            pltpu.VMEM((rows, width), bf16),
            pltpu.VMEM((HEAD_SIZE, COLS), bf16),
            pltpu.VMEM((HEAD_SIZE, COLS), f32),
            pltpu.VMEM((1, COLS), f32),
            pltpu.VMEM((1, COLS), f32),
            pltpu.VMEM((2, rows, COLS), bf16),
            pltpu.VMEM((rows, width), bf16),
            pltpu.VMEM(down_weight.shape, bf16),
            pltpu.VMEM(up_weight.shape, bf16),
            pltpu.VMEM((rows, width), bf16),
            pltpu.VMEM((8, 128), f32),
            pltpu.VMEM((3, 8, 128), f32),
            pltpu.VMEM((2, 8, 128), f32),
            pltpu.SMEM((SLOTS,), jnp.int32),
            pltpu.SMEM(patch_blocks.shape, jnp.int32),
            pltpu.SMEM(question_adapter.shape, jnp.int32),
            pltpu.SMEM(suffix_token_length.shape, jnp.int32),
            dma((9,)),
            dma((SLOTS, 2)),
            dma((SLOTS, 2)),
            dma((3, SLOTS)),
            dma((3, SLOTS)),
            dma((3,)),
            dma((3,)),
            dma((3,)),
            dma((3,)),
            dma((4,)),
            dma((4,)),
            pltpu.SemaphoreType.REGULAR,
            pltpu.SemaphoreType.REGULAR,
        ],
        compiler_params=pltpu.CompilerParams(
            collective_id=0, has_side_effects=True, vmem_limit_bytes=56 << 20
        ),
    )(
        patch_blocks,
        question_adapter,
        suffix_token_length,
        visual_key_value,
        queries.reshape(rows, width),
        suffix_key_value.reshape(asked, positions, -1),
        suffix_hidden_state.reshape(rows, width),
        down_weight,
        up_weight,
    )
    return result.reshape(queries.shape)


def solution(mesh):
    placed = (
        P(None, "seq", "enc", "tp"),
        P("enc", None),
        P("enc", "seq", None, "tp"),
        P("enc", "seq", None, "tp"),
        P("enc", "seq", None, "tp"),
        P("tp", None),
        P(None, "tp"),
        P("enc", "seq"),
        P("enc", "seq"),
    )
    return jax.shard_map(
        per_device,
        mesh=mesh,
        in_specs=placed,
        out_specs=P("enc", "seq", None, "tp"),
        check_vma=False,
    )
```

```python
import math

import jax
import jax.numpy as jnp
from jax import lax
from jax.experimental import pallas as pl
from jax.experimental.pallas import tpu as pltpu
from jax.sharding import PartitionSpec as P

MESH = pl.DeviceIdType.MESH
HEAD_SIZE = 128
ADAPTER_RANK = 16
ADAPTER_SCALE = 2.0
NEG_BIG = -1e30
NX, NZ, NY = 4, 4, 4
SLOTS = NX * NZ
GROUP = 4
KEYS = GROUP * 64
COLS = 1024
BLOCK = 128
EXP2_SCALE = math.log2(math.e) / math.sqrt(HEAD_SIZE)
HERE = [(0, 0), (1, 0), (3, 0), (2, 0)]
NEAR = [(dx, dz) for dx in (0, 1, 3, 2) for dz in (1, 3)]
FAR = [(dx, 2) for dx in (2, 3, 1, 0)]
OFFSETS = HERE + NEAR + FAR
FIRST_FAR = len(HERE + NEAR)
LATE = GROUP + 1
HELD = SLOTS - 2


def spread(rows):
    for shift in (64, 32, 16):
        rows = rows + pltpu.roll(rows, shift, 1)
    return rows


def kernel(
    blocks,
    adapter,
    length,
    visual,
    queries,
    suffix,
    hidden,
    down,
    up,
    out,
    kv,
    sx,
    qx,
    qfull,
    qt,
    acc,
    peak,
    total,
    res,
    hidden_v,
    down_v,
    up_v,
    queries_v,
    tp_send,
    tp_recv,
    len_tile,
    source_of,
    blocks_ref,
    adapter_ref,
    length_ref,
    load_sem,
    a2a_send,
    a2a_recv,
    y_send,
    y_recv,
    tp_ssem,
    tp_rsem,
    sib_ssem,
    sib_rsem,
    out_ssem,
    out_rsem,
    kept_sem,
    far_ready,
    pair_ready,
):
    e, s, t = lax.axis_index("enc"), lax.axis_index("seq"), lax.axis_index("tp")
    x, z = e // NZ, e % NZ
    y, c = s // 2, s % 2
    oc = 1 - c

    def enc_at(dx, dz):
        return ((x + dx) % NX) * NZ + (z + dz) % NZ

    def y_at(dy):
        return (e, ((y + dy) % NY) * 2 + c, t)

    sibling = (e, y * 2 + oc, t)

    barrier = pltpu.get_barrier_semaphore()
    peers = [sibling, y_at(1), y_at(2), y_at(3)]
    peers += [(e, s, (t + k) % 4) for k in (1, 2, 3)]
    for dx, dz in (HERE + NEAR)[1:]:
        peers.append((enc_at(dx, dz), s, t))
    for peer in peers:
        pl.semaphore_signal(barrier, inc=1, device_id=peer, device_id_type=MESH)

    loads = [
        pltpu.make_async_copy(src, dst, load_sem.at[i])
        for i, (src, dst) in enumerate(
            ((hidden, hidden_v), (down, down_v), (up, up_v), (queries, queries_v))
        )
    ]
    for load in loads:
        load.start()
    scalars = [
        pltpu.make_async_copy(src, dst, load_sem.at[6 + i])
        for i, (src, dst) in enumerate(
            ((blocks, blocks_ref), (adapter, adapter_ref), (length, length_ref))
        )
    ]
    for load in scalars:
        load.start()
    own_cols = pl.ds(pl.multiple_of(c * 256, 256), 256)
    sib_cols = pl.ds(pl.multiple_of(oc * 256, 256), 256)
    own_tile = pltpu.make_async_copy(
        visual.at[e, :, :, own_cols], kv.at[0, 0, pl.ds(2 * c, 2)], load_sem.at[4]
    )
    own_tile.start()
    own_suffix = pltpu.make_async_copy(
        suffix.at[:, :, own_cols], sx.at[c], load_sem.at[5]
    )
    own_suffix.start()

    for j, (dx, dz) in enumerate(OFFSETS):
        source_of[j] = enc_at(NX - dx, NZ - dz)

    lane = lax.broadcasted_iota(jnp.int32, (8, 128), 1)
    for load in [loads[0], loads[1], *scalars]:
        load.wait()
    lowered = jnp.dot(hidden_v[...], down_v[...], preferred_element_type=jnp.float32)
    packed = jnp.zeros((8, 128), jnp.float32)
    for g in range(8):
        own_adapter = adapter_ref[0, g // 4]
        rows = jnp.where(lane // ADAPTER_RANK == own_adapter, lowered[8 * g : 8 * g + 8], 0.0)
        packed = jnp.where(lane // ADAPTER_RANK == g, spread(rows), packed)
    tp_send[...] = packed
    len_tile[c] = jnp.where((lane // 32) % 2 == 0, length_ref[0, 0], length_ref[0, 1]).astype(
        jnp.float32
    )

    pl.semaphore_wait(barrier, len(peers))

    pl.semaphore_signal(pair_ready, inc=1, device_id=sibling, device_id_type=MESH)

    def remote(src, dst, ssem, rsem, device):
        return pltpu.make_async_remote_copy(
            src_ref=src,
            dst_ref=dst,
            send_sem=ssem,
            recv_sem=rsem,
            device_id=device,
            device_id_type=MESH,
        )

    tp_copies = [
        remote(
            tp_send, tp_recv.at[k - 1], tp_ssem.at[k - 1], tp_rsem.at[k - 1], (e, s, (t + k) % 4)
        )
        for k in (1, 2, 3)
    ]
    for copy in tp_copies:
        copy.start()

    def tile_send(dx, dz, j, core, cols):
        target = enc_at(dx, dz)
        return remote(
            visual.at[target, :, :, cols],
            kv.at[0, j, pl.ds(2 * c, 2)],
            a2a_send.at[j, core],
            a2a_recv.at[j, c],
            (target, y * 2 + core, t),
        )

    tile_send(0, 0, 0, oc, sib_cols).start()
    suffix_copy = remote(
        suffix.at[:, :, sib_cols], sx.at[c], sib_ssem.at[0], sib_rsem.at[0], sibling
    )
    suffix_copy.start()
    len_copy = remote(len_tile.at[c], len_tile.at[c], sib_ssem.at[1], sib_rsem.at[1], sibling)
    len_copy.start()
    for j in range(1, GROUP + 2):
        tile_send(*OFFSETS[j], j, c, own_cols).start()
    pl.semaphore_wait(pair_ready, 1)
    for j in range(1, GROUP + 2):
        tile_send(*OFFSETS[j], j, oc, sib_cols).start()
    for j in range(GROUP + 2, FIRST_FAR):
        tile_send(*OFFSETS[j], j, c, own_cols).start()
        tile_send(*OFFSETS[j], j, oc, sib_cols).start()
    pl.semaphore_signal(
        far_ready, inc=1, device_id=(enc_at(0, NZ - 1), s, t), device_id_type=MESH
    )

    def far_sends():
        for j in range(FIRST_FAR, SLOTS):
            tile_send(*OFFSETS[j], j, c, own_cols).start()
            tile_send(*OFFSETS[j], j, oc, sib_cols).start()

    inner = (t == 1) | (t == 2)

    def tile_wait(j, core):
        dst = kv.at[0, j, pl.ds(2 * core, 2)]
        remote(dst, dst, a2a_send.at[j, core], a2a_recv.at[j, core], sibling).wait_recv()

    def y_copy(way, j):
        return remote(
            kv.at[0, j],
            kv.at[1 + way, j],
            y_send.at[way, j],
            y_recv.at[way, j],
            y_at(1 if way == 0 else 3),
        )

    def y_relay(j):
        way = j % 2
        return remote(
            kv.at[1 + way, j],
            kv.at[3, j],
            y_send.at[2, j],
            y_recv.at[2, j],
            (e, ((y + 1 + 2 * way) % NY) * 2 + c, t),
        )

    def y_across(j):
        return remote(
            kv.at[0, j], kv.at[3, j], y_send.at[2, j], y_recv.at[2, j], y_at(2)
        )

    def y_wait(way, j):
        dst = kv.at[1 + way, j]
        remote(dst, dst, y_send.at[way, j], y_recv.at[way, j], sibling).wait_recv()

    def forward(j):
        y_copy(0, j).start()
        y_copy(1, j).start()

    def relay(j):
        y_wait(j % 2, j)
        y_relay(j).start()

    own_tile.wait()
    tile_wait(0, oc)
    forward(0)

    pl.semaphore_wait(far_ready, 1)

    @pl.when(inner)
    def _():
        far_sends()

    for copy in tp_copies:
        copy.wait_recv()
    packed = tp_send[...] + tp_recv[0] + tp_recv[1] + tp_recv[2]
    picked = []
    for g in range(8):
        own_adapter = adapter_ref[0, g // 4]
        rows = spread(jnp.where(lane // ADAPTER_RANK == g, packed, 0.0))
        picked.append(jnp.where(lane // ADAPTER_RANK == own_adapter, rows, 0.0))
    picked = jnp.concatenate(picked, axis=0).astype(jnp.bfloat16)
    loads[2].wait()
    loads[3].wait()
    for n in range(8):
        at = slice(n * 256, (n + 1) * 256)
        raised = jnp.dot(picked, up_v[:, at], preferred_element_type=jnp.float32)
        qfull[:, at] = (
            queries_v[:, at].astype(jnp.float32) + ADAPTER_SCALE * raised
        ).astype(jnp.bfloat16)
    own_half = pl.ds(pl.multiple_of(c * COLS, COLS), COLS)
    sib_half = pl.ds(pl.multiple_of(oc * COLS, COLS), COLS)
    query_copy = remote(
        qfull.at[:, sib_half], qx.at[c], sib_ssem.at[2], sib_rsem.at[2], sibling
    )
    query_copy.start()
    qx[c] = qfull[:, own_half]

    for j in range(1, GROUP):
        tile_wait(j, 0)
        tile_wait(j, 1)
        forward(j)
    for j in range(2):
        relay(j)

    for index, dst in ((0, sx.at[oc]), (1, len_tile.at[oc]), (2, qx.at[oc])):
        remote(dst, dst, sib_ssem.at[index], sib_rsem.at[index], sibling).wait_recv()
    own_suffix.wait()

    for g in range(8):
        rows = qx[:, :, g * 128 : (g + 1) * 128].reshape(128, 128)
        qt[:, g * 128 : (g + 1) * 128] = rows.T

    lengths = jnp.where(lane // 64 == 0, len_tile[0], len_tile[1])[0:1].astype(jnp.int32)
    key_at = lax.broadcasted_iota(jnp.int32, (128, 128), 0)
    col_at = lax.broadcasted_iota(jnp.int32, (128, 128), 1)
    limit = jnp.minimum(col_at % 32, lengths - 1)
    seen = (key_at // 32 == col_at // 32) & (key_at % 32 <= limit)
    keys = sx[:, :, :, 0:128].reshape(128, 128)
    values_t = sx[:, :, :, 128:256].reshape(128, 128).T
    for g in range(8):
        at = slice(g * 128, (g + 1) * 128)
        scores = jnp.dot(keys, qt[:, at], preferred_element_type=jnp.float32)
        scores = jnp.where(seen, scores, NEG_BIG)
        top = scores.max(axis=0, keepdims=True)
        weights = jnp.where(seen, jnp.exp2((scores - top) * EXP2_SCALE), 0.0)
        peak[:, at] = top
        total[:, at] = weights.sum(axis=0, keepdims=True)
        acc[:, at] = jnp.dot(
            values_t, weights.astype(jnp.bfloat16), preferred_element_type=jnp.float32
        )

    def attend(r, g):
        tile = kv.at[r, pl.ds(g * GROUP, GROUP)]
        keys = tile[:, :, :, 0:128].reshape(KEYS, 128)
        values_t = tile[:, :, :, 128:256].reshape(KEYS, 128).T
        from_y = (y + jnp.where(r == 0, 0, jnp.where(r == 1, 3, jnp.where(r == 2, 1, 2)))) % NY
        bias = []
        for i in range(GROUP * 4):
            held = blocks_ref[0, from_y * 4 + i % 4]
            live = source_of[g * GROUP + i // 4] < 2 * held
            bias.append(jnp.where(live, 0.0, NEG_BIG))
        for b in range(COLS // BLOCK):
            at = slice(b * BLOCK, (b + 1) * BLOCK)
            scores = jnp.dot(keys, qt[:, at], preferred_element_type=jnp.float32)
            before = peak[:, at]
            top = None
            for i in range(GROUP * 4):
                low, high = scores[16 * i : 16 * i + 8], scores[16 * i + 8 : 16 * i + 16]
                part = jnp.maximum(low, high) + bias[i]
                top = part if top is None else jnp.maximum(top, part)
            top = jnp.maximum(before, top.max(axis=0, keepdims=True))
            shrink = jnp.exp2((before - top) * EXP2_SCALE)
            scaled_top = top * EXP2_SCALE
            parts = []
            added = jnp.zeros((8, BLOCK), jnp.float32)
            for i in range(GROUP * 4):
                part = jnp.exp2(scores[16 * i : 16 * i + 16] * EXP2_SCALE - (scaled_top - bias[i]))
                added = added + (part[:8] + part[8:])
                parts.append(part.astype(jnp.bfloat16))
            peak[:, at] = top
            total[:, at] = total[:, at] * shrink + added.sum(axis=0, keepdims=True)
            acc[:, at] = acc[:, at] * shrink + jnp.dot(
                values_t, jnp.concatenate(parts, axis=0), preferred_element_type=jnp.float32
            )

    def step(k, _):
        @pl.when(k < SLOTS)
        def _():
            tile_wait(k, 0)
            tile_wait(k, 1)
            forward(k)

        @pl.when((k >= FIRST_FAR) & (k < SLOTS))
        def _():
            y_across(k).start()

        @pl.when((k == LATE) & jnp.logical_not(inner))
        def _():
            far_sends()

        @pl.when(k < FIRST_FAR + 2)
        def _():
            relay(k - 2)

        @pl.when((k < HELD) | (k >= SLOTS))
        def _():
            unit = jnp.where(k < SLOTS, k - GROUP, k - GROUP - (SLOTS - HELD))
            g, r = unit // 4, unit % 4
            for i in range(GROUP):
                j = g * GROUP + i

                @pl.when((r == 2 - i % 2) | ((r > 0) & (j >= FIRST_FAR)) | (r == 3))
                def _():
                    y_wait(r - 1, j)

            attend(r, g)

        return 0

    lax.fori_loop(GROUP, SLOTS + GROUP + (SLOTS - HELD), step, 0)

    keep = lax.broadcasted_iota(jnp.int32, (1, 128), 1) % 32 < lengths
    out_copies, kept_copies = [], []
    for n in range(4):
        for g in (2 * n, 2 * n + 1):
            at = slice(g * 128, (g + 1) * 128)
            rows = jnp.where(keep, acc[:, at] * (1.0 / total[:, at]), 0.0)
            rows = rows.astype(jnp.bfloat16).T
            res[:, :, at] = rows.reshape(2, 64, 128)
        half = pl.ds(pl.multiple_of(c * COLS + n * 256, 256), 256)
        copy = remote(
            res.at[oc, :, n * 256 : (n + 1) * 256],
            out.at[:, half],
            out_ssem.at[n],
            out_rsem.at[n],
            sibling,
        )
        copy.start()
        out_copies.append(copy)
        kept = pltpu.make_async_copy(
            res.at[c, :, n * 256 : (n + 1) * 256], out.at[:, half], kept_sem.at[n]
        )
        kept.start()
        kept_copies.append(kept)

    def drain(j, _):
        for core in (0, 1):

            @pl.when((j > 0) | (core == oc))
            def _():
                src = kv.at[0, j, pl.ds(2 * core, 2)]
                remote(src, src, a2a_send.at[j, core], a2a_recv.at[j, core], sibling).wait_send()

        for way in (0, 1, 2):
            src = kv.at[1 + way, j]
            remote(src, src, y_send.at[way, j], y_recv.at[way, j], sibling).wait_send()
        return 0

    lax.fori_loop(0, SLOTS, drain, 0)
    for copy in tp_copies + [suffix_copy, len_copy, query_copy]:
        copy.wait_send()
    for kept in kept_copies:
        kept.wait()
    for n, copy in enumerate(out_copies):
        copy.wait_send()
        arrived = out.at[:, pl.ds(pl.multiple_of(oc * COLS + n * 256, 256), 256)]
        remote(arrived, arrived, out_ssem.at[n], out_rsem.at[n], sibling).wait_recv()


def per_device(
    visual_key_value,
    patch_blocks,
    queries,
    suffix_key_value,
    suffix_hidden_state,
    down_weight,
    up_weight,
    question_adapter,
    suffix_token_length,
):
    bf16, f32 = jnp.bfloat16, jnp.float32
    asked, positions, width = queries.shape[1:]
    rows = asked * positions
    dma = pltpu.SemaphoreType.DMA
    hbm = pl.BlockSpec(memory_space=pl.ANY)
    result = pl.pallas_call(
        kernel,
        name="attention",
        out_shape=jax.ShapeDtypeStruct((rows, width), bf16),
        in_specs=[hbm] * 9,
        out_specs=hbm,
        scratch_shapes=[
            pltpu.VMEM((4, SLOTS, 4, 16, 256), bf16),
            pltpu.VMEM((2, 2, 32, 256), bf16),
            pltpu.VMEM((2, rows, COLS), bf16),
            pltpu.VMEM((rows, width), bf16),
            pltpu.VMEM((HEAD_SIZE, COLS), bf16),
            pltpu.VMEM((HEAD_SIZE, COLS), f32),
            pltpu.VMEM((1, COLS), f32),
            pltpu.VMEM((1, COLS), f32),
            pltpu.VMEM((2, rows, COLS), bf16),
            pltpu.VMEM((rows, width), bf16),
            pltpu.VMEM(down_weight.shape, bf16),
            pltpu.VMEM(up_weight.shape, bf16),
            pltpu.VMEM((rows, width), bf16),
            pltpu.VMEM((8, 128), f32),
            pltpu.VMEM((3, 8, 128), f32),
            pltpu.VMEM((2, 8, 128), f32),
            pltpu.SMEM((SLOTS,), jnp.int32),
            pltpu.SMEM(patch_blocks.shape, jnp.int32),
            pltpu.SMEM(question_adapter.shape, jnp.int32),
            pltpu.SMEM(suffix_token_length.shape, jnp.int32),
            dma((9,)),
            dma((SLOTS, 2)),
            dma((SLOTS, 2)),
            dma((3, SLOTS)),
            dma((3, SLOTS)),
            dma((3,)),
            dma((3,)),
            dma((3,)),
            dma((3,)),
            dma((4,)),
            dma((4,)),
            dma((4,)),
            pltpu.SemaphoreType.REGULAR,
            pltpu.SemaphoreType.REGULAR,
        ],
        compiler_params=pltpu.CompilerParams(
            collective_id=0, has_side_effects=True, vmem_limit_bytes=56 << 20
        ),
    )(
        patch_blocks,
        question_adapter,
        suffix_token_length,
        visual_key_value,
        queries.reshape(rows, width),
        suffix_key_value.reshape(asked, positions, -1),
        suffix_hidden_state.reshape(rows, width),
        down_weight,
        up_weight,
    )
    return result.reshape(queries.shape)


def solution(mesh):
    placed = (
        P(None, "seq", "enc", "tp"),
        P("enc", None),
        P("enc", "seq", None, "tp"),
        P("enc", "seq", None, "tp"),
        P("enc", "seq", None, "tp"),
        P("tp", None),
        P(None, "tp"),
        P("enc", "seq"),
        P("enc", "seq"),
    )
    return jax.shard_map(
        per_device,
        mesh=mesh,
        in_specs=placed,
        out_specs=P("enc", "seq", None, "tp"),
        check_vma=False,
    )
```
